32 devices in a mesh: chan: 8 (over z, y), win: 4 (over x, core).
Axes of the slice: x: 2, y: 2, z: 4, core: 2. Of those that a mesh axis runs over, the one named last changes fastest.
Arguments:
- strain: float32 [64, 32, 7500], P('chan', 'win'), may hold values from -800 to 800
- sources: int32 [4, 8], replicated, may hold values from 0 to 63, as said below
Outputs:
- stacks: float32 [32, 64, 513], P('win', 'chan')
The draws below stay inside these ranges and needn't reach their ends.
Inputs may be any that keep to these rules, and one draw needn't show every extreme that they name: `sources`: counting channels in aligned blocks of 8, the 8 channels of one round lie in different blocks, and over all rounds every block holds exactly 4 of them.
All inputs are finite; a program needn't handle non-finite values.
Results may differ from the reference program's by a relative error of at most 0.0024.
Values may be sent and summed in bfloat16 or wider, within the bound.
A program may use at most 128 MiB of HBM per device.

```python
import math
import jax
import jax.numpy as jnp
from jax import lax

CH_DEV = 8
SAMPLES = 7500
MAX_LAG = 256
SOURCES = 8
ROUNDS = 4
CHANNELS = 64
WINDOWS = 32


def draw_sources(key, part):
    owner_count = CHANNELS // CH_DEV
    shuffled = jax.random.permutation(jax.random.fold_in(key, 11), owner_count)
    owner_shards = shuffled[jnp.arange(ROUNDS * SOURCES) % owner_count]
    offsets = jax.random.randint(jax.random.fold_in(key, 12), (ROUNDS * SOURCES,), 0, CH_DEV)
    return (owner_shards * CH_DEV + offsets).astype(jnp.int32).reshape(ROUNDS, SOURCES)


def draw_strain(key, part):
    array_shape = (CHANNELS, WINDOWS, SAMPLES)
    envelope = jnp.exp(jax.random.uniform(jax.random.fold_in(key, 21), (1, WINDOWS, SAMPLES), jnp.float32) * math.log(10.0))
    row_level = jnp.exp(jax.random.uniform(jax.random.fold_in(key, 25), (CHANNELS, WINDOWS, 1), jnp.float32) * math.log(10.0))
    rough_part = jax.random.truncated_normal(jax.random.fold_in(key, 26), -4.0, 4.0, array_shape, jnp.float32)
    return row_level * envelope * rough_part


def setup_inputs(seed: int = 0) -> dict:
    keys = jax.random.split(jax.random.key(seed), 3)
    return {
        "strain": draw_strain(jax.random.fold_in(keys[2], 71), 0),
        "sources": draw_sources(jax.random.fold_in(keys[2], 71), 0),
    }


def whiten(strain):
    mean_square = lax.optimization_barrier(jnp.mean(strain * strain, axis=-1, keepdims=True))
    return (strain * lax.rsqrt(mean_square + 1e-06)).astype(jnp.bfloat16)

def receiver_rows(whitened, block_len):
    channels, windows, samples = whitened.shape
    blocks = -(-samples // block_len)
    padded = jnp.pad(whitened, ((0, 0), (0, 0), (0, blocks * block_len - samples)))
    pieces = padded.reshape(channels, windows, blocks, block_len)
    return jnp.transpose(pieces, (0, 3, 1, 2)).reshape(channels * block_len, windows * blocks)

def probe_columns(probe_rows, block_len, lag_blocks, max_lag):
    windows, samples = probe_rows.shape
    blocks = -(-samples // block_len)
    extent = (blocks + lag_blocks + 1) * block_len
    padded = jnp.pad(probe_rows, ((0, 0), (max_lag, extent - max_lag - samples)))
    pieces = padded.reshape(windows, blocks + lag_blocks + 1, block_len)
    stacked = jnp.stack([pieces[:, offset:offset + blocks, :] for offset in range(lag_blocks + 1)], axis=2)
    return stacked.reshape(windows * blocks, (lag_blocks + 1) * block_len)

def shear_sum(products, channels, block_len, lag_count):
    column_count = products.shape[1]
    flattened = products.reshape(channels, block_len * column_count)
    flattened = jnp.pad(flattened, ((0, 0), (0, block_len)))
    sheared = flattened.reshape(channels, block_len, column_count + 1)
    return lax.optimization_barrier(jnp.sum(sheared[:, :, :lag_count], axis=1))

def reference(strain, sources):
    whitened = whiten(strain)
    block_len = 64
    lag_count = 2 * MAX_LAG + 1
    lag_blocks = -(-lag_count // block_len)
    rows = receiver_rows(whitened, block_len).astype(jnp.float32)
    factor = 1.0 / math.sqrt(WINDOWS * SAMPLES)

    def correlate(channel):
        probe_rows = lax.dynamic_index_in_dim(whitened, channel, 0, keepdims=False)
        columns = probe_columns(probe_rows, block_len, lag_blocks, MAX_LAG).astype(jnp.float32)
        products = jnp.dot(rows, columns, precision=lax.Precision.HIGHEST, preferred_element_type=jnp.float32)
        return shear_sum(products, CHANNELS, block_len, lag_count) * factor
    return lax.map(correlate, sources.reshape(-1).astype(jnp.int32))
```

```python
import functools
import math

import jax
import jax.numpy as jnp
import ml_dtypes
import numpy as np
from jax import lax
from jax.experimental import pallas as pl
from jax.experimental.pallas import tpu as pltpu
from jax.sharding import PartitionSpec as P

MAX_LAG = 256
BLOCK = 128


def whiten(strain):
    mean_square = jnp.mean(strain * strain, axis=-1, keepdims=True)
    return (strain * lax.rsqrt(mean_square + 1e-06)).astype(jnp.bfloat16)


def ring_position(index, size):
    odd = lax.rem(index, 2)
    half = index // 2
    return (1 - odd) * half + odd * (size - 1 - half)


def ring_index(position, size):
    back = position // (size // 2)
    return (1 - back) * 2 * position + back * (2 * (size - 1 - position) + 1)


def kernel(
    sizes, streamed, factor, pieces_ref, local_ref, order_ref, out_ref,
    recv_ref, wide_ref, held_ref, own_ref, probe_ref, partial_ref, send_ref, land_ref,
    send_sem, recv_sem, stack_send_sem, stack_recv_sem,
):
    chan_size, win_size, lag_blocks, windows, front = sizes
    channels = recv_ref.shape[0]
    ways, _, count, depth, _ = held_ref.shape
    per_shard = ways * count
    here = ring_position(lax.axis_index("chan"), chan_size)
    win = lax.axis_index("win")
    right = ring_index(lax.rem(here + 1, chan_size), chan_size)
    left = ring_index(lax.rem(here + chan_size - 1, chan_size), chan_size)
    targets = [right, left]

    barrier = pltpu.get_barrier_semaphore()
    for chan in targets:
        pl.semaphore_signal(barrier, inc=1, device_id={"chan": chan}, device_id_type=pl.DeviceIdType.MESH)
    for step in range(1, win_size):
        peer = lax.rem(win + step, win_size)
        pl.semaphore_signal(barrier, inc=1, device_id={"win": peer}, device_id_type=pl.DeviceIdType.MESH)
    for way in range(ways):
        for item in range(count):
            held_ref[way, 0, item] = pieces_ref[local_ref[way * count + item]]
    own_ref[...] = jnp.zeros_like(own_ref)
    probe_ref[...] = jnp.zeros_like(probe_ref)
    pl.semaphore_wait(barrier, len(targets) + win_size - 1)

    row = lax.broadcasted_iota(jnp.int32, (BLOCK, BLOCK), 0)
    lane = lax.broadcasted_iota(jnp.int32, (BLOCK, BLOCK), 1)
    later = row + lane >= BLOCK - 1
    diagonal = row + lane == BLOCK - 1

    def hop(way, step, item):
        return pltpu.make_async_remote_copy(
            src_ref=held_ref.at[way, step, item],
            dst_ref=held_ref.at[way, step + 1, item],
            send_sem=send_sem.at[way, step, item],
            recv_sem=recv_sem.at[way, step, item],
            device_id={"chan": targets[way]},
            device_id_type=pl.DeviceIdType.MESH,
        )

    def stack_hop(dest, origin):
        slot = lax.rem(dest - win + win_size, win_size) - 1
        return pltpu.make_async_remote_copy(
            src_ref=partial_ref.at[origin * per_shard + dest],
            dst_ref=land_ref.at[slot, origin],
            send_sem=stack_send_sem.at[dest, origin],
            recv_sem=stack_recv_sem.at[slot, origin],
            device_id={"win": jnp.int32(dest)},
            device_id_type=pl.DeviceIdType.MESH,
        )

    def origin_of(way, step):
        position = here - step if way == 0 else here + step
        return ring_index(lax.rem(position + chan_size, chan_size), chan_size)

    def load(probe, item, step):
        for way in range(ways):
            probe[item, :depth, way * BLOCK : (way + 1) * BLOCK] = held_ref[way, step, item]

    def work(probe, item, step, channel):
        products = jnp.dot(recv_ref[channel], probe[item], preferred_element_type=jnp.float32)
        for way in range(ways):
            columns = products[:, way * BLOCK : (way + 1) * BLOCK]
            parts = [columns[k * BLOCK : (k + 1) * BLOCK] for k in range(lag_blocks + 1)]
            totals = []
            for k in range(lag_blocks):
                mixed = jnp.where(later, parts[k], parts[k + 1])
                sheared = pltpu.roll(mixed, 0, 1, stride=1, stride_axis=0)
                total = jnp.sum(sheared, axis=0, keepdims=True)
                totals.append(pltpu.roll(total, 1, 1) * factor)
            last = jnp.where(diagonal, parts[lag_blocks], 0.0)
            last = jnp.sum(jnp.sum(last, axis=0, keepdims=True), axis=1, keepdims=True)
            totals.append(jnp.broadcast_to(last * factor, (1, BLOCK)))
            place = origin_of(way, step) * per_shard + way * count + item
            partial_ref[place, pl.ds(channel, 1), :] = jnp.concatenate(totals, axis=1)

    def send_stacks(item, step):
        if not streamed:
            return
        for way in range(ways):
            dest = way * count + item

            @pl.when(win != dest)
            def _():
                stack_hop(dest, origin_of(way, step)).start()

    for way in range(ways):
        for item in range(count):
            hop(way, 0, item).start()

    reverse = jnp.where(diagonal, 1.0, 0.0).astype(jnp.bfloat16)
    inner = recv_ref.shape[2]
    reach = wide_ref.shape[1]
    wide_ref[...] = jnp.zeros_like(wide_ref)
    for channel in range(channels):
        wide_ref[channel % 2, front : front + depth, :] = pieces_ref[channel]
        flipped = lax.dot_general(
            reverse, wide_ref[channel % 2], (((1,), (1,)), ((), ())), preferred_element_type=jnp.float32
        )
        for k in range(lag_blocks + 1):
            shift = (lag_blocks - k) * windows
            moved = pltpu.roll(flipped, reach - shift, 1) if shift else flipped
            recv_ref[channel, k * BLOCK : (k + 1) * BLOCK, :] = moved[:, :inner].astype(jnp.bfloat16)

    spread = chan_size - 1 if chan_size - 1 <= channels else 0
    for item in range(count):
        load(own_ref, item, 0)
        for channel in range(channels - spread):
            work(own_ref, item, 0, channel)

    def body(step, carry):
        for item in range(count):
            for way in range(ways):
                hop(way, step - 1, item).wait_recv()

                @pl.when(step < chan_size - 1)
                def _():
                    hop(way, step, item).start()

            load(probe_ref, item, step)
            if spread:
                work(own_ref, item, 0, channels - spread + step - 1)
            for channel in range(channels):
                work(probe_ref, item, step, channel)
            send_stacks(item, step)
        return carry

    lax.fori_loop(1, chan_size, body, 0)
    for item in range(count):
        send_stacks(item, 0)
    for step in range(chan_size - 1):
        for way in range(ways):
            for item in range(count):
                hop(way, step, item).wait_send()

    per_win = out_ref.shape[0]
    if streamed:
        def arrived(index, carry):
            for slot in range(win_size - 1):
                peer = lax.rem(win + slot + 1, win_size)
                pltpu.make_async_remote_copy(
                    src_ref=partial_ref.at[index],
                    dst_ref=land_ref.at[slot, index],
                    send_sem=stack_send_sem.at[slot, index],
                    recv_sem=stack_recv_sem.at[slot, index],
                    device_id={"win": peer},
                    device_id_type=pl.DeviceIdType.MESH,
                ).wait_recv()
            return carry

        lax.fori_loop(0, chan_size, arrived, 0)
        for item in range(per_win):
            place = order_ref[win * per_win + item]
            owner = lax.div(place, per_shard)
            total = partial_ref[place]
            for slot in range(win_size - 1):
                total = total + land_ref[slot, owner]
            out_ref[item] = total[:, : out_ref.shape[2]]

        def sent(index, carry):
            for dest in range(win_size):
                @pl.when(win != dest)
                def _():
                    stack_hop(dest, index).wait_send()
            return carry

        lax.fori_loop(0, chan_size, sent, 0)
        return

    for dest in range(win_size):
        for item in range(per_win):
            send_ref[dest, item] = partial_ref[order_ref[dest * per_win + item]]

    def stack_copy(step):
        peer = lax.rem(win + step, win_size)
        return pltpu.make_async_remote_copy(
            src_ref=send_ref.at[peer],
            dst_ref=land_ref.at[step - 1],
            send_sem=stack_send_sem.at[step - 1],
            recv_sem=stack_recv_sem.at[step - 1],
            device_id={"win": peer},
            device_id_type=pl.DeviceIdType.MESH,
        )

    for step in range(1, win_size):
        stack_copy(step).start()
    for step in range(1, win_size):
        stack_copy(step).wait_recv()
    total = send_ref[win]
    for step in range(1, win_size):
        total = total + land_ref[step - 1]
    out_ref[...] = total[:, :, : out_ref.shape[2]]
    for step in range(1, win_size):
        stack_copy(step).wait_send()


def correlate(pieces, local_channel, order, windows, rounds, factor):
    channels, depth, _ = pieces.shape
    per_shard = local_channel.shape[0]
    total = order.shape[0]
    chan_size, win_size = lax.axis_size("chan"), lax.axis_size("win")
    lag_blocks = 2 * MAX_LAG // BLOCK
    lag_count = 2 * MAX_LAG + 1
    front = (lag_blocks - MAX_LAG // BLOCK) * windows
    inner = -(-depth // 256) * 256
    reach = -(-(inner + lag_blocks * windows) // BLOCK) * BLOCK
    lanes = (lag_blocks + 1) * BLOCK
    per_win = total // win_size
    streamed = rounds == win_size and total // rounds == chan_size and per_shard == rounds
    stack_copies = (win_size, chan_size) if streamed else (win_size - 1,)
    ways = 2 if per_shard % 2 == 0 else 1
    count = per_shard // ways
    return pl.pallas_call(
        functools.partial(kernel, (chan_size, win_size, lag_blocks, windows, front), streamed, factor),
        out_shape=jax.ShapeDtypeStruct((per_win, channels, lag_count), jnp.float32),
        in_specs=[
            pl.BlockSpec(memory_space=pltpu.VMEM),
            pl.BlockSpec(memory_space=pltpu.SMEM),
            pl.BlockSpec(memory_space=pltpu.SMEM),
        ],
        out_specs=pl.BlockSpec(memory_space=pltpu.VMEM),
        scratch_shapes=[
            pltpu.VMEM((channels, (lag_blocks + 1) * BLOCK, inner), jnp.bfloat16),
            pltpu.VMEM((2, reach, BLOCK), jnp.bfloat16),
            pltpu.VMEM((ways, chan_size, count, depth, BLOCK), jnp.bfloat16),
            pltpu.VMEM((count, inner, ways * BLOCK), jnp.bfloat16),
            pltpu.VMEM((count, inner, ways * BLOCK), jnp.bfloat16),
            pltpu.VMEM((total, channels, lanes), jnp.float32),
            pltpu.VMEM((win_size, per_win, channels, lanes), jnp.float32),
            pltpu.VMEM((win_size - 1, per_win, channels, lanes), jnp.float32),
            pltpu.SemaphoreType.DMA((ways, chan_size - 1, count)),
            pltpu.SemaphoreType.DMA((ways, chan_size - 1, count)),
            pltpu.SemaphoreType.DMA(stack_copies),
            pltpu.SemaphoreType.DMA(stack_copies),
        ],
        compiler_params=pltpu.CompilerParams(
            vmem_limit_bytes=48 * 1024 * 1024, collective_id=0, has_side_effects=True
        ),
    )(pieces, local_channel, order)


STEP = 32
QUAD = BLOCK // STEP
TAPS = MAX_LAG // STEP
POINTS = 3 * TAPS
TONES = POINTS // 2
LAGS = 2 * MAX_LAG // STEP + 1
HALO = MAX_LAG // BLOCK


def tones():
    return 2 * np.pi * (np.arange(TONES) + 0.5) / POINTS


def wave_rows():
    angle = np.outer(tones(), np.arange(POINTS))
    rows = np.stack([np.cos(angle), -np.sin(angle)], axis=1)
    scales = np.linspace(1.0, 2.0, 2000, endpoint=False)
    kept, used = [], []
    for row in rows:
        scaled = scales[:, None, None] * row
        near = scaled.astype(ml_dtypes.bfloat16).astype(np.float64)
        error = np.sum((near / scales[:, None, None] - row) ** 2, axis=(1, 2))
        best = int(np.argmin(error))
        kept.append(near[best])
        used.append(scales[best])
    return np.array(kept), np.array(used)


def constants(windows, channels, factor):
    rows, scales = wave_rows()
    bf16 = ml_dtypes.bfloat16
    perm = np.zeros((QUAD, QUAD, STEP, QUAD, STEP, QUAD), np.float32)
    for o in range(QUAD):
        for q in range(QUAD):
            perm[o, q, np.arange(STEP), q, np.arange(STEP), o] = 1
    perm = perm.reshape(QUAD * BLOCK, QUAD * BLOCK)
    parts = channels // QUAD
    turn = np.zeros((STEP, parts, QUAD, parts, STEP, QUAD), np.float32)
    for part in range(parts):
        for c in range(QUAD):
            turn[np.arange(STEP), part, c, part, np.arange(STEP), c] = 1
    turn = turn.reshape(STEP * channels, STEP * channels)
    eye = np.eye(windows)

    def dft(taps):
        blocks = (taps + TAPS) // QUAD
        out = np.zeros((TONES, 2, 2, windows, QUAD, blocks, windows))
        for seg in range(2):
            for n in range(taps):
                place = seg * TAPS + n
                out[:, :, seg, :, place % QUAD, place // QUAD, :] = rows[:, :, n, None, None] * eye
        return out.reshape(TONES * 4 * windows, QUAD * blocks * windows)

    phase = np.repeat(np.outer(tones(), np.arange(STEP) / STEP), QUAD, axis=1)
    twist = np.stack([np.cos(phase), np.sin(phase)], axis=1)
    twist = np.broadcast_to(twist[:, :, None, :], (TONES, 2, 8, BLOCK))
    angle = np.outer(np.arange(LAGS), tones())
    back = np.stack([np.cos(angle), -np.sin(angle)], axis=2) * (factor / TONES / scales**2)[:, None]
    inverse = np.einsum("kfv,cd->kcfvd", back, np.eye(channels)).reshape(LAGS * channels, TONES * 2 * channels)
    return (
        jnp.asarray(perm.astype(bf16)),
        jnp.asarray(turn.astype(bf16)),
        jnp.asarray(dft(TAPS).astype(bf16)),
        jnp.asarray(dft(POINTS).astype(bf16)),
        jnp.asarray(np.ascontiguousarray(twist).astype(np.float32)),
        jnp.asarray(inverse.astype(np.float32)),
    )


def halves_kernel(
    windows, pieces_ref, sources_ref, perm_ref, turn_ref, dft_a_ref, dft_b_ref, twist_ref, inverse_ref, out_ref,
    pair_ref, own_ref, pick_ref, held_ref, xa_ref, sa_ref, a_ref, xb_ref, sb_ref, spec_ref, res_ref, land_ref,
    half_ref, part_ref, fin_ref,
    pair_sem, far_send, far_recv, side_send, side_recv, stack_send, stack_recv, end_sem,
):
    channels, depth, _ = pieces_ref.shape
    rounds, per_round = sources_ref.shape
    rows = held_ref.shape[3]
    halo = HALO * windows
    span = depth // 2
    size = span + halo
    pairs = sb_ref.shape[1] // 2 // (2 * windows)
    two = 2 * windows
    chan = lax.axis_index("chan")
    win = lax.axis_index("win")
    z, y = lax.div(chan, 2), lax.rem(chan, 2)
    half = lax.rem(z, 2)
    pair_z = z + 1 - 2 * half
    far = [lax.rem(z - half + 2 + k, QUAD) for k in range(2)]
    order = [z, pair_z] + far
    MESH = pl.DeviceIdType.MESH

    def source_rows(h):
        return pl.ds(pl.multiple_of(h * (span - halo), 16), size)

    def held_rows(h):
        return pl.ds(pl.multiple_of((1 - h) * halo, 16), size)

    def round_at(step):
        return lax.rem(win + 1 + step, rounds)

    def channel_of(step, shard):
        found = jnp.int32(0)
        for i in range(per_round):
            source = sources_ref[round_at(step), i]
            found += jnp.where(source // channels == shard, source - shard * channels, 0)
        return found

    barrier = pltpu.get_barrier_semaphore()
    edge = jnp.zeros((16, BLOCK), jnp.bfloat16)
    edges = [*range(0, halo, 16), *range(size, rows, 16)]
    for at in edges:
        for step in range(rounds):
            for side in range(2):
                for zz in range(QUAD):
                    held_ref[step, side, zz, at : at + 16, :] = edge
        for c in range(channels):
            pair_ref[c, at : at + 16, :] = edge
            own_ref[c, at : at + 16, :] = edge
    peers = [{"chan": pair_z * 2 + y}, {"chan": far[0] * 2 + y}, {"chan": far[1] * 2 + y}, {"chan": z * 2 + 1 - y}]
    peers += [{"win": lax.rem(win + 1 + step, rounds)} for step in range(rounds - 1)]
    for peer in peers:
        pl.semaphore_signal(barrier, inc=1, device_id=peer, device_id_type=MESH)

    pair_copy = pltpu.make_async_remote_copy(
        src_ref=pieces_ref.at[:, source_rows(1 - half), :],
        dst_ref=pair_ref.at[:, held_rows(1 - half), :],
        send_sem=pair_sem.at[0],
        recv_sem=pair_sem.at[1],
        device_id=peers[0],
        device_id_type=MESH,
    )

    def far_copy(step, k):
        return pltpu.make_async_remote_copy(
            src_ref=pick_ref.at[step, source_rows(k), :],
            dst_ref=held_ref.at[step, 0, z, held_rows(k), :],
            send_sem=far_send.at[step, k],
            recv_sem=far_recv.at[step, half],
            device_id=peers[1 + k],
            device_id_type=MESH,
        )

    def far_wait(step, k):
        pltpu.make_async_remote_copy(
            src_ref=pick_ref.at[step, source_rows(half), :],
            dst_ref=held_ref.at[step, 0, far[k], held_rows(half), :],
            send_sem=far_send.at[step, k],
            recv_sem=far_recv.at[step, k],
            device_id=peers[1 + k],
            device_id_type=MESH,
        ).wait_recv()

    def side_copy(step, o):
        return pltpu.make_async_remote_copy(
            src_ref=held_ref.at[step, 0, order[o], held_rows(half), :],
            dst_ref=held_ref.at[step, 1, order[o], held_rows(half), :],
            send_sem=side_send.at[step, o],
            recv_sem=side_recv.at[step, o],
            device_id=peers[3],
            device_id_type=MESH,
        )

    def stack_copy(step):
        return pltpu.make_async_remote_copy(
            src_ref=res_ref.at[step],
            dst_ref=land_ref.at[step],
            send_sem=stack_send.at[step],
            recv_sem=stack_recv.at[step],
            device_id={"win": lax.rem(win + 1 + step, rounds)},
            device_id_type=MESH,
        )

    end_copy = pltpu.make_async_remote_copy(
        src_ref=half_ref,
        dst_ref=part_ref,
        send_sem=end_sem.at[0],
        recv_sem=end_sem.at[1],
        device_id=peers[0],
        device_id_type=MESH,
    )

    for step in range(rounds):
        pick_ref[step] = pieces_ref[channel_of(step, chan)]
        held_ref[step, 0, z, held_rows(half), :] = pick_ref[step, source_rows(half), :]
    for c in range(channels):
        own_ref[c, held_rows(half), :] = pieces_ref[c, source_rows(half), :]
    pl.semaphore_wait(barrier, len(peers))
    for k in range(2):
        far_copy(0, k).start()
    pair_copy.start()
    for step in range(rounds):
        side_copy(step, 0).start()
        if step:
            for k in range(2):
                far_copy(step, k).start()

    def twisted(real, imag, f):
        cos, sin = twist_ref[f, 0], twist_ref[f, 1]
        reals, imags = [], []
        for part in range(real.shape[1] // BLOCK):
            lanes = slice(part * BLOCK, (part + 1) * BLOCK)
            turned = []
            for at in range(0, real.shape[0], 8):
                re, im = real[at : at + 8, lanes], imag[at : at + 8, lanes]
                turned.append((re * cos + im * sin, im * cos - re * sin))
            reals.append(jnp.concatenate([t[0] for t in turned], axis=0))
            imags.append(jnp.concatenate([t[1] for t in turned], axis=0))
        return jnp.concatenate(reals, axis=1).astype(jnp.bfloat16), jnp.concatenate(imags, axis=1).astype(jnp.bfloat16)

    def spread(refs, at, count, put):
        joined = jnp.concatenate([r[at : at + count, :] for r in refs], axis=1)
        put(jnp.dot(joined, perm_ref[...], preferred_element_type=jnp.float32).astype(jnp.bfloat16))

    def receivers(which, ref):
        for part in range(channels // QUAD):
            def put(value):
                for q in range(QUAD):
                    xa_ref[q, 0:span, part * BLOCK : (part + 1) * BLOCK] = value[:, q * BLOCK : (q + 1) * BLOCK]

            spread([ref.at[part * QUAD + o] for o in range(QUAD)], halo, span, put)

        def waves(g, carry):
            at = pl.multiple_of(g * two * TAPS // QUAD, 16)
            taken = jnp.concatenate([xa_ref[q, pl.ds(at, two * TAPS // QUAD), :] for q in range(QUAD)], axis=0)
            seen = jnp.dot(dft_a_ref[...], taken, preferred_element_type=jnp.float32)
            here = pl.multiple_of(g * two, 16)
            for f in range(TONES):
                real, imag = twisted(seen[2 * f * two : (2 * f + 1) * two], seen[(2 * f + 1) * two : (2 * f + 2) * two], f)
                sa_ref[f, 0, pl.ds(here, two), :] = real
                sa_ref[f, 1, pl.ds(here, two), :] = imag
            return carry

        lax.fori_loop(0, pairs, waves, 0)
        wide = pairs * two

        def turned(f, carry):
            real, imag = [
                lax.dot_general(
                    turn_ref[...], sa_ref[f, v], (((1,), (1,)), ((), ())), preferred_element_type=jnp.float32
                ).astype(jnp.bfloat16)
                for v in range(2)
            ]
            a_ref[which, f, 0, :, 0:wide] = real
            a_ref[which, f, 0, :, wide : 2 * wide] = imag
            a_ref[which, f, 1, :, 0:wide] = -imag
            a_ref[which, f, 1, :, wide : 2 * wide] = real
            return carry

        lax.fori_loop(0, TONES, turned, 0)

    def sources(step):
        wide = pairs * two
        for side in range(2):
            def put(value):
                for q in range(QUAD):
                    xb_ref[q, :, side * BLOCK : (side + 1) * BLOCK] = value[:, q * BLOCK : (q + 1) * BLOCK]

            spread([held_ref.at[step, side, zz] for zz in range(QUAD)], 0, rows, put)

        def waves(g, carry):
            count = windows * (TAPS + POINTS) // QUAD
            at = pl.multiple_of(g * two * TAPS // QUAD, 16)
            taken = jnp.concatenate([xb_ref[q, pl.ds(at, count), :] for q in range(QUAD)], axis=0)
            seen = jnp.dot(dft_b_ref[...], taken, preferred_element_type=jnp.float32)
            here = pl.multiple_of(g * two, 16)
            for f in range(TONES):
                real, imag = twisted(seen[2 * f * two : (2 * f + 1) * two], seen[(2 * f + 1) * two : (2 * f + 2) * two], f)
                sb_ref[f, pl.ds(here, two), :] = real
                sb_ref[f, pl.ds(pl.multiple_of(here + wide, 16), two), :] = imag
            return carry

        lax.fori_loop(0, pairs, waves, 0)

    def products(step):
        def tone(f, carry):
            right = sb_ref[f]
            for which in range(2):
                sums = []
                for v in range(2):
                    seen = jnp.dot(a_ref[which, f, v], right, preferred_element_type=jnp.float32)
                    for side in range(2):
                        lanes = slice(side * BLOCK, (side + 1) * BLOCK)
                        total = [None] * 4
                        for i in range(STEP):
                            term = seen[i * channels : (i + 1) * channels, lanes]
                            if i:
                                term = pltpu.roll(term, BLOCK - QUAD * i, 1)
                            total[i % 4] = term if total[i % 4] is None else total[i % 4] + term
                        sums.append((total[0] + total[1]) + (total[2] + total[3]))
                cos, sin = twist_ref[f, 0], twist_ref[f, 1]
                at = pl.multiple_of(f * 2 * channels, 16)
                for side in range(2):
                    lanes = slice(side * BLOCK, (side + 1) * BLOCK)
                    re, im = sums[side], sums[2 + side]
                    both = jnp.concatenate([re * cos - im * sin, re * sin + im * cos], axis=0)
                    spec_ref[which, pl.ds(at, 2 * channels), lanes] = both
            return carry

        lax.fori_loop(0, TONES, tone, 0)
        for which in range(2):
            res_ref[step, which] = jnp.dot(
                inverse_ref[...], spec_ref[which], precision=lax.Precision.HIGHEST, preferred_element_type=jnp.float32
            )

    xa_ref[:, span:, :] = jnp.zeros((QUAD, xa_ref.shape[1] - span, xa_ref.shape[2]), jnp.bfloat16)
    receivers(0, own_ref)
    pair_copy.wait_recv()
    for step in range(rounds):
        channel = channel_of(step, pair_z * 2 + y)
        held_ref[step, 0, pair_z, held_rows(half), :] = pair_ref[channel, held_rows(half), :]
        side_copy(step, 1).start()
    receivers(1, pair_ref)

    def pass_on(step):
        for k in range(2):
            far_wait(step, k)
            side_copy(step, 2 + k).start()

    pass_on(0)

    def body(step, carry):
        for o in range(QUAD):
            side_copy(step, o).wait_recv()
        sources(step)

        @pl.when(step < rounds - 1)
        def _():
            pass_on(step + 1)

        products(step)

        @pl.when(step < rounds - 1)
        def _():
            stack_copy(step).start()

        return carry

    lax.fori_loop(0, rounds, body, 0)

    for step in range(rounds - 1):
        stack_copy(step).wait_recv()
    sums = []
    for which in range(2):
        total = res_ref[rounds - 1, which]
        for step in range(rounds - 1):
            total = total + land_ref[step, which]
        if which == 0:
            sums.append(total)
        else:
            half_ref[...] = total
    end_copy.start()
    for step in range(rounds):
        for k in range(2):
            far_copy(step, k).wait_send()
        for o in range(QUAD):
            side_copy(step, o).wait_send()
    pair_copy.wait_send()
    for step in range(rounds - 1):
        stack_copy(step).wait_send()
    end_copy.wait_recv()
    total = sums[0] + part_ref[...]
    groups = (LAGS - 1) // QUAD
    for side in range(2):
        lanes = slice(side * BLOCK, (side + 1) * BLOCK)
        lined = jnp.concatenate(
            [
                jnp.concatenate(
                    [total[(QUAD * g + q) * channels : (QUAD * g + q + 1) * channels, lanes] for g in range(groups)], axis=0
                )
                for q in range(QUAD)
            ],
            axis=1,
        )
        high = lined.astype(jnp.bfloat16)
        rest = lined - high.astype(jnp.float32)
        middle = rest.astype(jnp.bfloat16)
        low = (rest - middle.astype(jnp.float32)).astype(jnp.bfloat16)
        split = [
            lax.dot_general(p, perm_ref[...], (((1,), (1,)), ((), ())), preferred_element_type=jnp.float32)
            for p in (high, middle, low)
        ]
        whole = split[0] + split[1] + split[2]
        last = total[(LAGS - 1) * channels : LAGS * channels, lanes]
        for zz in range(QUAD):
            for g in range(groups):
                fin_ref[side * QUAD + zz, :, g * BLOCK : (g + 1) * BLOCK] = whole[
                    g * channels : (g + 1) * channels, zz * BLOCK : (zz + 1) * BLOCK
                ]
            fin_ref[side * QUAD + zz, :, groups * BLOCK : (groups + 1) * BLOCK] = jnp.broadcast_to(
                last[:, zz : zz + 1], (channels, BLOCK)
            )
    for i in range(per_round):
        shard = sources_ref[win, i] // channels
        side = jnp.where(shard - 2 * (shard // 2) == y, 0, 1)
        out_ref[i] = fin_ref[side * QUAD + shard // 2][:, : out_ref.shape[2]]
    end_copy.wait_send()


def halves_fit(channels, windows, blocks, rounds, per_round):
    chan_size, win_size = lax.axis_size("chan"), lax.axis_size("win")
    return (
        rounds == win_size
        and per_round == chan_size
        and chan_size == 2 * QUAD
        and win_size == QUAD
        and channels == 2 * QUAD
        and windows == 8
        and blocks % 4 == 0
    )


def correlate_halves(pieces, sources, factor):
    channels, depth, _ = pieces.shape
    rounds, per_round = sources.shape
    windows = 8
    tables = constants(windows, channels, factor)
    span = depth // 2
    pairs = -(-span // (windows * 4))
    rows = (pairs * 4 + 2 * HALO) * windows
    wide = channels * STEP
    stack = (LAGS * channels, 2 * BLOCK)
    bf16, f32 = jnp.bfloat16, jnp.float32
    dma = pltpu.SemaphoreType.DMA
    return pl.pallas_call(
        functools.partial(halves_kernel, windows),
        out_shape=jax.ShapeDtypeStruct((per_round, channels, 2 * MAX_LAG + 1), f32),
        in_specs=[pl.BlockSpec(memory_space=pltpu.VMEM), pl.BlockSpec(memory_space=pltpu.SMEM)]
        + [pl.BlockSpec(memory_space=pltpu.VMEM)] * len(tables),
        out_specs=pl.BlockSpec(memory_space=pltpu.VMEM),
        scratch_shapes=[
            pltpu.VMEM((channels, rows, BLOCK), bf16),
            pltpu.VMEM((channels, rows, BLOCK), bf16),
            pltpu.VMEM((rounds, depth, BLOCK), bf16),
            pltpu.VMEM((rounds, 2, QUAD, rows, BLOCK), bf16),
            pltpu.VMEM((QUAD, pairs * 4 * windows, wide), bf16),
            pltpu.VMEM((TONES, 2, pairs * 2 * windows, wide), bf16),
            pltpu.VMEM((2, TONES, 2, wide, pairs * 4 * windows), bf16),
            pltpu.VMEM((QUAD, rows, 2 * BLOCK), bf16),
            pltpu.VMEM((TONES, pairs * 4 * windows, 2 * BLOCK), bf16),
            pltpu.VMEM((2, TONES * 2 * channels, 2 * BLOCK), f32),
            pltpu.VMEM((rounds, 2, *stack), f32),
            pltpu.VMEM((rounds - 1, 2, *stack), f32),
            pltpu.VMEM(stack, f32),
            pltpu.VMEM(stack, f32),
            pltpu.VMEM((per_round, channels, 2 * MAX_LAG + BLOCK), f32),
            dma((2,)),
            dma((rounds, 2)),
            dma((rounds, 2)),
            dma((rounds, QUAD)),
            dma((rounds, QUAD)),
            dma((rounds - 1,)),
            dma((rounds - 1,)),
            dma((2,)),
        ],
        compiler_params=pltpu.CompilerParams(
            vmem_limit_bytes=48 * 1024 * 1024, collective_id=1, has_side_effects=True
        ),
    )(pieces, sources, *tables)


def on_device(strain, sources):
    channels, windows, samples = strain.shape
    rounds, per_round = sources.shape
    total_sources = rounds * per_round
    factor = 1.0 / math.sqrt(lax.axis_size("win") * windows * samples)
    blocks = -(-samples // BLOCK)
    while blocks * windows % 16:
        blocks += 1
    depth = blocks * windows

    whitened = whiten(strain)
    padded = jnp.pad(whitened, ((0, 0), (0, 0), (0, blocks * BLOCK - samples)))
    pieces = padded.reshape(channels, windows, blocks, BLOCK)
    pieces = jnp.transpose(pieces, (0, 2, 1, 3)).reshape(channels, depth, BLOCK)

    if halves_fit(channels, windows, blocks, rounds, per_round):
        return correlate_halves(pieces, sources.astype(jnp.int32), factor)

    flat_sources = sources.reshape(-1)
    per_shard = total_sources // lax.axis_size("chan")
    owner = flat_sources // channels
    position = jnp.arange(total_sources)
    earlier = (owner[None, :] == owner[:, None]) & (position[None, :] < position[:, None])
    rank = jnp.sum(earlier.astype(jnp.int32), axis=1)
    me = lax.axis_index("chan")
    mine = owner == me
    slot_pick = (mine[None, :] & (rank[None, :] == jnp.arange(per_shard)[:, None])).astype(jnp.int32)
    local_channel = jnp.sum(slot_pick * (flat_sources - me * channels)[None, :], axis=1)
    order = (owner * per_shard + rank).astype(jnp.int32)

    return correlate(pieces, local_channel.astype(jnp.int32), order, windows, rounds, factor)


def solution(mesh):
    in_specs = (P("chan", "win", None), P())
    out_specs = P("win", "chan", None)
    return jax.shard_map(
        on_device, mesh=mesh, in_specs=in_specs, out_specs=out_specs, check_vma=False
    )
```

```python
import functools
import math

import jax
import jax.numpy as jnp
import ml_dtypes
import numpy as np
from jax import lax
from jax.experimental import pallas as pl
from jax.experimental.pallas import tpu as pltpu
from jax.sharding import PartitionSpec as P

MAX_LAG = 256
BLOCK = 128


def whiten(strain):
    mean_square = jnp.mean(strain * strain, axis=-1, keepdims=True)
    return (strain * lax.rsqrt(mean_square + 1e-06)).astype(jnp.bfloat16)


def ring_position(index, size):
    odd = lax.rem(index, 2)
    half = index // 2
    return (1 - odd) * half + odd * (size - 1 - half)


def ring_index(position, size):
    back = position // (size // 2)
    return (1 - back) * 2 * position + back * (2 * (size - 1 - position) + 1)


def kernel(
    sizes, streamed, factor, pieces_ref, local_ref, order_ref, out_ref,
    recv_ref, wide_ref, held_ref, own_ref, probe_ref, partial_ref, send_ref, land_ref,
    send_sem, recv_sem, stack_send_sem, stack_recv_sem,
):
    chan_size, win_size, lag_blocks, windows, front = sizes
    channels = recv_ref.shape[0]
    ways, _, count, depth, _ = held_ref.shape
    per_shard = ways * count
    here = ring_position(lax.axis_index("chan"), chan_size)
    win = lax.axis_index("win")
    right = ring_index(lax.rem(here + 1, chan_size), chan_size)
    left = ring_index(lax.rem(here + chan_size - 1, chan_size), chan_size)
    targets = [right, left]

    barrier = pltpu.get_barrier_semaphore()
    for chan in targets:
        pl.semaphore_signal(barrier, inc=1, device_id={"chan": chan}, device_id_type=pl.DeviceIdType.MESH)
    for step in range(1, win_size):
        peer = lax.rem(win + step, win_size)
        pl.semaphore_signal(barrier, inc=1, device_id={"win": peer}, device_id_type=pl.DeviceIdType.MESH)
    for way in range(ways):
        for item in range(count):
            held_ref[way, 0, item] = pieces_ref[local_ref[way * count + item]]
    own_ref[...] = jnp.zeros_like(own_ref)
    probe_ref[...] = jnp.zeros_like(probe_ref)
    pl.semaphore_wait(barrier, len(targets) + win_size - 1)

    row = lax.broadcasted_iota(jnp.int32, (BLOCK, BLOCK), 0)
    lane = lax.broadcasted_iota(jnp.int32, (BLOCK, BLOCK), 1)
    later = row + lane >= BLOCK - 1
    diagonal = row + lane == BLOCK - 1

    def hop(way, step, item):
        return pltpu.make_async_remote_copy(
            src_ref=held_ref.at[way, step, item],
            dst_ref=held_ref.at[way, step + 1, item],
            send_sem=send_sem.at[way, step, item],
            recv_sem=recv_sem.at[way, step, item],
            device_id={"chan": targets[way]},
            device_id_type=pl.DeviceIdType.MESH,
        )

    def stack_hop(dest, origin):
        slot = lax.rem(dest - win + win_size, win_size) - 1
        return pltpu.make_async_remote_copy(
            src_ref=partial_ref.at[origin * per_shard + dest],
            dst_ref=land_ref.at[slot, origin],
            send_sem=stack_send_sem.at[dest, origin],
            recv_sem=stack_recv_sem.at[slot, origin],
            device_id={"win": jnp.int32(dest)},
            device_id_type=pl.DeviceIdType.MESH,
        )

    def origin_of(way, step):
        position = here - step if way == 0 else here + step
        return ring_index(lax.rem(position + chan_size, chan_size), chan_size)

    def load(probe, item, step):
        for way in range(ways):
            probe[item, :depth, way * BLOCK : (way + 1) * BLOCK] = held_ref[way, step, item]

    def work(probe, item, step, channel):
        products = jnp.dot(recv_ref[channel], probe[item], preferred_element_type=jnp.float32)
        for way in range(ways):
            columns = products[:, way * BLOCK : (way + 1) * BLOCK]
            parts = [columns[k * BLOCK : (k + 1) * BLOCK] for k in range(lag_blocks + 1)]
            totals = []
            for k in range(lag_blocks):
                mixed = jnp.where(later, parts[k], parts[k + 1])
                sheared = pltpu.roll(mixed, 0, 1, stride=1, stride_axis=0)
                total = jnp.sum(sheared, axis=0, keepdims=True)
                totals.append(pltpu.roll(total, 1, 1) * factor)
            last = jnp.where(diagonal, parts[lag_blocks], 0.0)
            last = jnp.sum(jnp.sum(last, axis=0, keepdims=True), axis=1, keepdims=True)
            totals.append(jnp.broadcast_to(last * factor, (1, BLOCK)))
            place = origin_of(way, step) * per_shard + way * count + item
            partial_ref[place, pl.ds(channel, 1), :] = jnp.concatenate(totals, axis=1)

    def send_stacks(item, step):
        if not streamed:
            return
        for way in range(ways):
            dest = way * count + item

            @pl.when(win != dest)
            def _():
                stack_hop(dest, origin_of(way, step)).start()

    for way in range(ways):
        for item in range(count):
            hop(way, 0, item).start()

    reverse = jnp.where(diagonal, 1.0, 0.0).astype(jnp.bfloat16)
    inner = recv_ref.shape[2]
    reach = wide_ref.shape[1]
    wide_ref[...] = jnp.zeros_like(wide_ref)
    for channel in range(channels):
        wide_ref[channel % 2, front : front + depth, :] = pieces_ref[channel]
        flipped = lax.dot_general(
            reverse, wide_ref[channel % 2], (((1,), (1,)), ((), ())), preferred_element_type=jnp.float32
        )
        for k in range(lag_blocks + 1):
            shift = (lag_blocks - k) * windows
            moved = pltpu.roll(flipped, reach - shift, 1) if shift else flipped
            recv_ref[channel, k * BLOCK : (k + 1) * BLOCK, :] = moved[:, :inner].astype(jnp.bfloat16)

    spread = chan_size - 1 if chan_size - 1 <= channels else 0
    for item in range(count):
        load(own_ref, item, 0)
        for channel in range(channels - spread):
            work(own_ref, item, 0, channel)

    def body(step, carry):
        for item in range(count):
            for way in range(ways):
                hop(way, step - 1, item).wait_recv()

                @pl.when(step < chan_size - 1)
                def _():
                    hop(way, step, item).start()

            load(probe_ref, item, step)
            if spread:
                work(own_ref, item, 0, channels - spread + step - 1)
            for channel in range(channels):
                work(probe_ref, item, step, channel)
            send_stacks(item, step)
        return carry

    lax.fori_loop(1, chan_size, body, 0)
    for item in range(count):
        send_stacks(item, 0)
    for step in range(chan_size - 1):
        for way in range(ways):
            for item in range(count):
                hop(way, step, item).wait_send()

    per_win = out_ref.shape[0]
    if streamed:
        def arrived(index, carry):
            for slot in range(win_size - 1):
                peer = lax.rem(win + slot + 1, win_size)
                pltpu.make_async_remote_copy(
                    src_ref=partial_ref.at[index],
                    dst_ref=land_ref.at[slot, index],
                    send_sem=stack_send_sem.at[slot, index],
                    recv_sem=stack_recv_sem.at[slot, index],
                    device_id={"win": peer},
                    device_id_type=pl.DeviceIdType.MESH,
                ).wait_recv()
            return carry

        lax.fori_loop(0, chan_size, arrived, 0)
        for item in range(per_win):
            place = order_ref[win * per_win + item]
            owner = lax.div(place, per_shard)
            total = partial_ref[place]
            for slot in range(win_size - 1):
                total = total + land_ref[slot, owner]
            out_ref[item] = total[:, : out_ref.shape[2]]

        def sent(index, carry):
            for dest in range(win_size):
                @pl.when(win != dest)
                def _():
                    stack_hop(dest, index).wait_send()
            return carry

        lax.fori_loop(0, chan_size, sent, 0)
        return

    for dest in range(win_size):
        for item in range(per_win):
            send_ref[dest, item] = partial_ref[order_ref[dest * per_win + item]]

    def stack_copy(step):
        peer = lax.rem(win + step, win_size)
        return pltpu.make_async_remote_copy(
            src_ref=send_ref.at[peer],
            dst_ref=land_ref.at[step - 1],
            send_sem=stack_send_sem.at[step - 1],
            recv_sem=stack_recv_sem.at[step - 1],
            device_id={"win": peer},
            device_id_type=pl.DeviceIdType.MESH,
        )

    for step in range(1, win_size):
        stack_copy(step).start()
    for step in range(1, win_size):
        stack_copy(step).wait_recv()
    total = send_ref[win]
    for step in range(1, win_size):
        total = total + land_ref[step - 1]
    out_ref[...] = total[:, :, : out_ref.shape[2]]
    for step in range(1, win_size):
        stack_copy(step).wait_send()


def correlate(pieces, local_channel, order, windows, rounds, factor):
    channels, depth, _ = pieces.shape
    per_shard = local_channel.shape[0]
    total = order.shape[0]
    chan_size, win_size = lax.axis_size("chan"), lax.axis_size("win")
    lag_blocks = 2 * MAX_LAG // BLOCK
    lag_count = 2 * MAX_LAG + 1
    front = (lag_blocks - MAX_LAG // BLOCK) * windows
    inner = -(-depth // 256) * 256
    reach = -(-(inner + lag_blocks * windows) // BLOCK) * BLOCK
    lanes = (lag_blocks + 1) * BLOCK
    per_win = total // win_size
    streamed = rounds == win_size and total // rounds == chan_size and per_shard == rounds
    stack_copies = (win_size, chan_size) if streamed else (win_size - 1,)
    ways = 2 if per_shard % 2 == 0 else 1
    count = per_shard // ways
    return pl.pallas_call(
        functools.partial(kernel, (chan_size, win_size, lag_blocks, windows, front), streamed, factor),
        out_shape=jax.ShapeDtypeStruct((per_win, channels, lag_count), jnp.float32),
        in_specs=[
            pl.BlockSpec(memory_space=pltpu.VMEM),
            pl.BlockSpec(memory_space=pltpu.SMEM),
            pl.BlockSpec(memory_space=pltpu.SMEM),
        ],
        out_specs=pl.BlockSpec(memory_space=pltpu.VMEM),
        scratch_shapes=[
            pltpu.VMEM((channels, (lag_blocks + 1) * BLOCK, inner), jnp.bfloat16),
            pltpu.VMEM((2, reach, BLOCK), jnp.bfloat16),
            pltpu.VMEM((ways, chan_size, count, depth, BLOCK), jnp.bfloat16),
            pltpu.VMEM((count, inner, ways * BLOCK), jnp.bfloat16),
            pltpu.VMEM((count, inner, ways * BLOCK), jnp.bfloat16),
            pltpu.VMEM((total, channels, lanes), jnp.float32),
            pltpu.VMEM((win_size, per_win, channels, lanes), jnp.float32),
            pltpu.VMEM((win_size - 1, per_win, channels, lanes), jnp.float32),
            pltpu.SemaphoreType.DMA((ways, chan_size - 1, count)),
            pltpu.SemaphoreType.DMA((ways, chan_size - 1, count)),
            pltpu.SemaphoreType.DMA(stack_copies),
            pltpu.SemaphoreType.DMA(stack_copies),
        ],
        compiler_params=pltpu.CompilerParams(
            vmem_limit_bytes=48 * 1024 * 1024, collective_id=0, has_side_effects=True
        ),
    )(pieces, local_channel, order)


STEP = 32
QUAD = BLOCK // STEP
TAPS = MAX_LAG // STEP
POINTS = 3 * TAPS
TONES = POINTS // 2
LAGS = 2 * MAX_LAG // STEP + 1
HALO = MAX_LAG // BLOCK


def tones():
    return 2 * np.pi * (np.arange(TONES) + 0.5) / POINTS


def wave_rows():
    angle = np.outer(tones(), np.arange(POINTS))
    rows = np.stack([np.cos(angle), -np.sin(angle)], axis=1)
    scales = np.linspace(1.0, 2.0, 2000, endpoint=False)
    kept, used = [], []
    for row in rows:
        scaled = scales[:, None, None] * row
        near = scaled.astype(ml_dtypes.bfloat16).astype(np.float64)
        error = np.sum((near / scales[:, None, None] - row) ** 2, axis=(1, 2))
        best = int(np.argmin(error))
        kept.append(near[best])
        used.append(scales[best])
    return np.array(kept), np.array(used)


def constants(windows, channels, factor):
    rows, scales = wave_rows()
    bf16 = ml_dtypes.bfloat16
    perm = np.zeros((QUAD, QUAD, STEP, QUAD, STEP, QUAD), np.float32)
    for o in range(QUAD):
        for q in range(QUAD):
            perm[o, q, np.arange(STEP), q, np.arange(STEP), o] = 1
    perm = perm.reshape(QUAD * BLOCK, QUAD * BLOCK)
    parts = channels // QUAD
    turn = np.zeros((STEP, parts, QUAD, parts, STEP, QUAD), np.float32)
    for part in range(parts):
        for c in range(QUAD):
            turn[np.arange(STEP), part, c, part, np.arange(STEP), c] = 1
    turn = turn.reshape(STEP * channels, STEP * channels)
    eye = np.eye(windows)

    def dft(taps):
        blocks = (taps + TAPS) // QUAD
        out = np.zeros((TONES, 2, 2, windows, QUAD, blocks, windows))
        for seg in range(2):
            for n in range(taps):
                place = seg * TAPS + n
                out[:, :, seg, :, place % QUAD, place // QUAD, :] = rows[:, :, n, None, None] * eye
        return out.reshape(TONES * 4 * windows, QUAD * blocks * windows)

    phase = np.repeat(np.outer(tones(), np.arange(STEP) / STEP), QUAD, axis=1)
    twist = np.stack([np.cos(phase), np.sin(phase)], axis=1)
    twist = np.broadcast_to(twist[:, :, None, :], (TONES, 2, 8, BLOCK))
    angle = np.outer(np.arange(LAGS), tones())
    back = np.stack([np.cos(angle), -np.sin(angle)], axis=2) * (factor / TONES / scales**2)[:, None]
    inverse = np.einsum("kfv,cd->kcfvd", back, np.eye(channels)).reshape(LAGS * channels, TONES * 2 * channels)
    return (
        jnp.asarray(perm.astype(bf16)),
        jnp.asarray(turn.astype(bf16)),
        jnp.asarray(dft(TAPS).astype(bf16)),
        jnp.asarray(dft(POINTS).astype(bf16)),
        jnp.asarray(np.ascontiguousarray(twist).astype(np.float32)),
        jnp.asarray(inverse.astype(np.float32)),
    )


def halves_kernel(
    windows, pieces_ref, sources_ref, perm_ref, turn_ref, dft_a_ref, dft_b_ref, twist_ref, inverse_ref, out_ref,
    near_ref, pair_ref, own_ref, pick_ref, held_ref, spun_ref, xa_ref, sa_ref, a_ref, xb_ref, sb_ref, spec_ref, res_ref, sent_ref, land_ref,
    half_ref, part_ref, fin_ref,
    pair_sem, far_send, far_recv, side_send, side_recv, stack_send, stack_recv, end_sem,
):
    channels, depth, _ = pieces_ref.shape
    rounds, per_round = sources_ref.shape
    rows = held_ref.shape[3]
    halo = HALO * windows
    span = depth // 2
    size = span + halo
    pairs = sb_ref.shape[2] // 4 // (2 * windows)
    two = 2 * windows
    chan = lax.axis_index("chan")
    win = lax.axis_index("win")
    z, y = lax.div(chan, 2), lax.rem(chan, 2)
    half = lax.rem(z, 2)
    pair_z = z + 1 - 2 * half
    far = [lax.rem(z - half + 2 + k, QUAD) for k in range(2)]
    order = [z, pair_z] + far
    MESH = pl.DeviceIdType.MESH

    def source_rows(h):
        return pl.ds(pl.multiple_of(h * (span - halo), 16), size)

    def held_rows(h):
        return pl.ds(pl.multiple_of((1 - h) * halo, 16), size)

    def round_at(step):
        return lax.rem(win + jnp.where(step == 0, 2, jnp.where(step == 1, 1, jnp.where(step == 2, 3, 0))), rounds)

    def channel_of(step, shard):
        found = jnp.int32(0)
        for i in range(per_round):
            source = sources_ref[round_at(step), i]
            found += jnp.where(source // channels == shard, source - shard * channels, 0)
        return found

    def plan(shard):
        wanted = [channel_of(step, shard) for step in range(rounds)]
        first = []
        for step in range(rounds):
            found = jnp.int32(step)
            for earlier in reversed(range(step)):
                found = jnp.where(wanted[earlier] == wanted[step], earlier, found)
            first.append(found)
        ranks, free = [], jnp.int32(0)
        for c in range(channels):
            taken = jnp.int32(0)
            for channel in wanted:
                taken = jnp.where(channel == c, 1, taken)
            ranks.append(jnp.where(taken == 1, -1, free))
            free = free + 1 - taken
        line, spare = [], jnp.int32(0)
        for place in range(channels):
            filler = jnp.int32(0)
            for c in range(channels):
                filler = jnp.where(ranks[c] == spare, c, filler)
            if place < rounds:
                repeated = jnp.where(first[place] == place, 0, 1)
                line.append(jnp.where(repeated == 1, filler, wanted[place]))
                spare = spare + repeated
            else:
                line.append(filler)
                spare = spare + 1
        return wanted, first, line

    barrier = pltpu.get_barrier_semaphore()
    edge = jnp.zeros((16, BLOCK), jnp.bfloat16)
    edges = [*range(0, halo, 16), *range(size, rows, 16)]
    for at in edges:
        for step in range(rounds):
            for side in range(2):
                for zz in range(QUAD):
                    held_ref[step, side, zz, at : at + 16, :] = edge
        for c in range(channels):
            pair_ref[c, at : at + 16, :] = edge
            own_ref[c, at : at + 16, :] = edge
    peers = [{"chan": pair_z * 2 + y}, {"chan": far[0] * 2 + y}, {"chan": far[1] * 2 + y}, {"chan": z * 2 + 1 - y}]
    peers += [{"win": lax.rem(win + 1 + step, rounds)} for step in range(rounds - 1)]
    for peer in peers:
        pl.semaphore_signal(barrier, inc=1, device_id=peer, device_id_type=MESH)

    def near_copy(place):
        return pltpu.make_async_remote_copy(
            src_ref=near_ref.at[place],
            dst_ref=pair_ref.at[place, held_rows(1 - half), :],
            send_sem=pair_sem.at[0, place],
            recv_sem=pair_sem.at[1, place],
            device_id=peers[0],
            device_id_type=MESH,
        )

    def near_wait(place):
        pltpu.make_async_remote_copy(
            src_ref=near_ref.at[place],
            dst_ref=pair_ref.at[place, held_rows(half), :],
            send_sem=pair_sem.at[0, place],
            recv_sem=pair_sem.at[1, place],
            device_id=peers[0],
            device_id_type=MESH,
        ).wait_recv()

    def far_copy(step, k):
        return pltpu.make_async_remote_copy(
            src_ref=pick_ref.at[step, source_rows(k), :],
            dst_ref=held_ref.at[step, 0, z, held_rows(k), :],
            send_sem=far_send.at[step, k],
            recv_sem=far_recv.at[step, half],
            device_id=peers[1 + k],
            device_id_type=MESH,
        )

    def far_wait(step, k):
        pltpu.make_async_remote_copy(
            src_ref=pick_ref.at[step, source_rows(half), :],
            dst_ref=held_ref.at[step, 0, far[k], held_rows(half), :],
            send_sem=far_send.at[step, k],
            recv_sem=far_recv.at[step, k],
            device_id=peers[1 + k],
            device_id_type=MESH,
        ).wait_recv()

    def side_copy(step, o):
        return pltpu.make_async_remote_copy(
            src_ref=held_ref.at[step, 0, order[o], held_rows(half), :],
            dst_ref=held_ref.at[step, 1, order[o], held_rows(half), :],
            send_sem=side_send.at[step, o],
            recv_sem=side_recv.at[step, o],
            device_id=peers[3],
            device_id_type=MESH,
        )

    def stack_copy(step, which):
        return pltpu.make_async_remote_copy(
            src_ref=sent_ref.at[step, which],
            dst_ref=land_ref.at[step, which],
            send_sem=stack_send.at[step, which],
            recv_sem=stack_recv.at[step, which],
            device_id={"win": round_at(step)},
            device_id_type=MESH,
        )

    end_copy = pltpu.make_async_remote_copy(
        src_ref=half_ref,
        dst_ref=part_ref,
        send_sem=end_sem.at[0],
        recv_sem=end_sem.at[1],
        device_id=peers[0],
        device_id_type=MESH,
    )

    wanted, _, line = plan(chan)
    for step in range(rounds):
        pick_ref[step] = pieces_ref[wanted[step]]
        held_ref[step, 0, z, held_rows(half), :] = pick_ref[step, source_rows(half), :]
    for place in range(channels):
        near_ref[place] = pieces_ref[line[place], source_rows(1 - half), :]
    pl.semaphore_wait(barrier, len(peers))
    ahead = [1, 2, 5, 8]
    sent = 0
    for step in range(rounds):
        for place in range(sent, ahead[step]):
            near_copy(place).start()
        sent = ahead[step]
        for k in range(2):
            far_copy(step, k).start()
    for step in range(rounds):
        side_copy(step, 0).start()
    for c in range(channels):
        own_ref[c, held_rows(half), :] = pieces_ref[c, source_rows(half), :]

    def twisted(real, imag, f):
        cos, sin = twist_ref[f, 0], twist_ref[f, 1]
        reals, imags = [], []
        for part in range(real.shape[1] // BLOCK):
            lanes = slice(part * BLOCK, (part + 1) * BLOCK)
            turned = []
            for at in range(0, real.shape[0], 8):
                re, im = real[at : at + 8, lanes], imag[at : at + 8, lanes]
                turned.append((re * cos + im * sin, im * cos - re * sin))
            reals.append(jnp.concatenate([t[0] for t in turned], axis=0))
            imags.append(jnp.concatenate([t[1] for t in turned], axis=0))
        return jnp.concatenate(reals, axis=1).astype(jnp.bfloat16), jnp.concatenate(imags, axis=1).astype(jnp.bfloat16)

    def half_turn(value):
        return pltpu.roll(value, BLOCK // 2, 1)

    def spread(refs, at, count, put):
        joined = jnp.concatenate([r[at : at + count, :] for r in refs], axis=1)
        put(jnp.dot(joined, perm_ref[...], preferred_element_type=jnp.float32).astype(jnp.bfloat16))

    def receivers(which, ref, spin_ref):
        for part in range(channels // QUAD):
            def put(value):
                for q in range(QUAD):
                    xa_ref[q, 0:span, part * BLOCK : (part + 1) * BLOCK] = value[:, q * BLOCK : (q + 1) * BLOCK]

            spread([ref.at[part * QUAD + o] for o in range(QUAD)], halo, span, put)

        def waves(g, carry):
            at = pl.multiple_of(g * two * TAPS // QUAD, 16)
            taken = jnp.concatenate([xa_ref[q, pl.ds(at, two * TAPS // QUAD), :] for q in range(QUAD)], axis=0)
            seen = jnp.dot(dft_a_ref[...], taken, preferred_element_type=jnp.float32)
            here = pl.multiple_of(g * two, 16)
            for f in range(TONES):
                real, imag = twisted(seen[2 * f * two : (2 * f + 1) * two], seen[(2 * f + 1) * two : (2 * f + 2) * two], f)
                sa_ref[f, 0, pl.ds(here, two), :] = real
                sa_ref[f, 1, pl.ds(here, two), :] = imag
            return carry

        lax.fori_loop(0, pairs, waves, 0, unroll=8)
        wide = pairs * two

        def turned(f, carry):
            real, imag = [
                lax.dot_general(
                    spin_ref[...], sa_ref[f, v], (((1,), (1,)), ((), ())), preferred_element_type=jnp.float32
                ).astype(jnp.bfloat16)
                for v in range(2)
            ]
            deep = STEP * channels // 2
            for u in range(2):
                at = 2 * u * wide
                re, im = real[u * deep : (u + 1) * deep], imag[u * deep : (u + 1) * deep]
                a_ref[which, f, 0, :, at : at + wide] = re
                a_ref[which, f, 0, :, at + wide : at + 2 * wide] = im
                a_ref[which, f, 1, :, at : at + wide] = -im
                a_ref[which, f, 1, :, at + wide : at + 2 * wide] = re
            return carry

        lax.fori_loop(0, TONES, turned, 0, unroll=12)

    def sources(step):
        wide = pairs * two
        for side in range(2):
            def put(value):
                for q in range(QUAD):
                    xb_ref[q, :, side * BLOCK : (side + 1) * BLOCK] = value[:, q * BLOCK : (q + 1) * BLOCK]

            spread([held_ref.at[step, side, zz] for zz in range(QUAD)], 0, rows, put)

        def waves(g, carry):
            count = windows * (TAPS + POINTS) // QUAD
            at = pl.multiple_of(g * two * TAPS // QUAD, 16)
            taken = jnp.concatenate([xb_ref[q, pl.ds(at, count), :] for q in range(QUAD)], axis=0)
            seen = jnp.dot(dft_b_ref[...], taken, preferred_element_type=jnp.float32)
            here = pl.multiple_of(g * two, 16)
            for f in range(TONES):
                real, imag = twisted(seen[2 * f * two : (2 * f + 1) * two], seen[(2 * f + 1) * two : (2 * f + 2) * two], f)
                for v, part in enumerate((real, imag)):
                    sb_ref[step, f, pl.ds(pl.multiple_of(here + v * wide, 16), two), :] = part
                    for side in range(2):
                        lanes = slice(side * BLOCK, (side + 1) * BLOCK)
                        sb_ref[step, f, pl.ds(pl.multiple_of(here + (v + 2) * wide, 16), two), lanes] = half_turn(part[:, lanes])
            return carry

        lax.fori_loop(0, pairs, waves, 0, unroll=8)

    def products(step, which):
        def tone(f, carry):
            right = sb_ref[step, f]
            sums = []
            for v in range(2):
                seen = jnp.dot(a_ref[which, f, v], right, preferred_element_type=jnp.float32)
                for side in range(2):
                    lanes = slice(side * BLOCK, (side + 1) * BLOCK)
                    total = [None] * 4
                    for i in range(STEP // 2):
                        term = seen[i * channels : (i + 1) * channels, lanes]
                        if i:
                            term = pltpu.roll(term, BLOCK - QUAD * i, 1)
                        total[i % 4] = term if total[i % 4] is None else total[i % 4] + term
                    sums.append((total[0] + total[1]) + (total[2] + total[3]))
            cos, sin = twist_ref[f, 0], twist_ref[f, 1]
            at = pl.multiple_of(f * 2 * channels, 16)
            for side in range(2):
                lanes = slice(side * BLOCK, (side + 1) * BLOCK)
                re, im = sums[side], sums[2 + side]
                both = jnp.concatenate([re * cos - im * sin, re * sin + im * cos], axis=0)
                spec_ref[which, pl.ds(at, 2 * channels), lanes] = both
            return carry

        lax.fori_loop(0, TONES, tone, 0, unroll=12)
        sums = jnp.dot(
            inverse_ref[...], spec_ref[which], precision=lax.Precision.HIGHEST, preferred_element_type=jnp.float32
        )
        sums = jnp.concatenate([sums[:, :BLOCK], sums[:, BLOCK:]], axis=0)
        res_ref[which] = sums
        sent_ref[step, which] = sums.astype(jnp.bfloat16)

    _, first, pair_line = plan(pair_z * 2 + y)

    def pass_on(step):
        if step < 3:
            near_wait(step)
        total = pair_ref[0, held_rows(half), :]
        if step:
            total = jnp.zeros(total.shape, jnp.float32)
            for place in range(step + 1):
                share = jnp.where(first[step] == place, 1.0, 0.0)
                total = total + pair_ref[place, held_rows(half), :].astype(jnp.float32) * share
            total = total.astype(jnp.bfloat16)
        held_ref[step, 0, pair_z, held_rows(half), :] = total
        side_copy(step, 1).start()
        for k in range(2):
            far_wait(step, k)
            side_copy(step, 2 + k).start()

    def take(step):
        for o in range(QUAD):
            side_copy(step, o).wait_recv()
        sources(step)

    xa_ref[:, span:, :] = jnp.zeros((QUAD, xa_ref.shape[1] - span, xa_ref.shape[2]), jnp.bfloat16)
    receivers(0, own_ref, turn_ref)
    row = lax.broadcasted_iota(jnp.int32, spun_ref.shape, 0)
    lane = lax.broadcasted_iota(jnp.int32, spun_ref.shape, 1)
    place = lane // BLOCK * QUAD + lane % QUAD
    meant = jnp.zeros_like(lane)
    for c in range(channels):
        meant = jnp.where(place == c, pair_line[c], meant)
    hit = (lane % BLOCK // QUAD * channels + meant) == row
    spun_ref[...] = jnp.where(hit, 1.0, 0.0).astype(jnp.bfloat16)
    pass_on(0)
    pass_on(1)

    def early(step, carry):
        take(step)
        products(step, 0)
        stack_copy(step, 0).start()

        @pl.when(step == 0)
        def _():
            pass_on(2)

        return carry

    lax.fori_loop(0, 2, early, 0)
    for place in range(3, channels):
        near_wait(place)
    receivers(1, pair_ref, spun_ref)

    def shared(step, carry):
        products(step, 1)
        stack_copy(step, 1).start()
        return carry

    lax.fori_loop(0, 2, shared, 0)
    pass_on(3)

    def late(step, carry):
        take(step)

        def each(index, carry):
            products(step, 1 - index)

            @pl.when(step < rounds - 1)
            def _():
                stack_copy(step, 1 - index).start()

            return carry

        lax.fori_loop(0, 2, each, 0)
        return carry

    lax.fori_loop(2, rounds, late, 0)
    totals = []
    for which in (1, 0):
        total = res_ref[which]
        for step in range(rounds - 1):
            stack_copy(step, which).wait_recv()
            total = total + land_ref[step, which].astype(jnp.float32)
        totals.append(total)
        if which:
            half_ref[...] = total.astype(jnp.bfloat16)
            end_copy.start()
    for step in range(rounds):
        for k in range(2):
            far_copy(step, k).wait_send()
        for o in range(QUAD):
            side_copy(step, o).wait_send()
    for place in range(channels):
        near_copy(place).wait_send()
    for step in range(rounds - 1):
        for which in range(2):
            stack_copy(step, which).wait_send()
    end_copy.wait_recv()
    both = totals[1] + part_ref[...].astype(jnp.float32)
    groups = (LAGS - 1) // QUAD
    for side in range(2):
        total = both[side * LAGS * channels : (side + 1) * LAGS * channels]
        lined = jnp.concatenate(
            [
                jnp.concatenate(
                    [total[(QUAD * g + q) * channels : (QUAD * g + q + 1) * channels] for g in range(groups)], axis=0
                )
                for q in range(QUAD)
            ],
            axis=1,
        )
        high = lined.astype(jnp.bfloat16)
        rest = lined - high.astype(jnp.float32)
        middle = rest.astype(jnp.bfloat16)
        low = (rest - middle.astype(jnp.float32)).astype(jnp.bfloat16)
        split = [
            lax.dot_general(p, perm_ref[...], (((1,), (1,)), ((), ())), preferred_element_type=jnp.float32)
            for p in (high, middle, low)
        ]
        whole = split[0] + split[1] + split[2]
        last = total[(LAGS - 1) * channels : LAGS * channels]
        for zz in range(QUAD):
            for g in range(groups):
                fin_ref[side * QUAD + zz, :, g * BLOCK : (g + 1) * BLOCK] = whole[
                    g * channels : (g + 1) * channels, zz * BLOCK : (zz + 1) * BLOCK
                ]
            fin_ref[side * QUAD + zz, :, groups * BLOCK : (groups + 1) * BLOCK] = jnp.broadcast_to(
                last[:, zz : zz + 1], (channels, BLOCK)
            )
    for i in range(per_round):
        shard = sources_ref[win, i] // channels
        side = jnp.where(shard - 2 * (shard // 2) == y, 0, 1)
        out_ref[i] = fin_ref[side * QUAD + shard // 2][:, : out_ref.shape[2]]
    end_copy.wait_send()


def halves_fit(channels, windows, blocks, rounds, per_round):
    chan_size, win_size = lax.axis_size("chan"), lax.axis_size("win")
    return (
        rounds == win_size
        and per_round == chan_size
        and chan_size == 2 * QUAD
        and win_size == QUAD
        and channels == 2 * QUAD
        and windows == 8
        and blocks % 4 == 0
    )


def correlate_halves(pieces, sources, factor):
    channels, depth, _ = pieces.shape
    rounds, per_round = sources.shape
    windows = 8
    tables = constants(windows, channels, factor)
    span = depth // 2
    pairs = -(-span // (windows * 4))
    rows = (pairs * 4 + 2 * HALO) * windows
    wide = channels * STEP
    stack = (2 * LAGS * channels, BLOCK)
    bf16, f32 = jnp.bfloat16, jnp.float32
    dma = pltpu.SemaphoreType.DMA
    return pl.pallas_call(
        functools.partial(halves_kernel, windows),
        out_shape=jax.ShapeDtypeStruct((per_round, channels, 2 * MAX_LAG + 1), f32),
        in_specs=[pl.BlockSpec(memory_space=pltpu.VMEM), pl.BlockSpec(memory_space=pltpu.SMEM)]
        + [pl.BlockSpec(memory_space=pltpu.VMEM)] * len(tables),
        out_specs=pl.BlockSpec(memory_space=pltpu.VMEM),
        scratch_shapes=[
            pltpu.VMEM((channels, span + HALO * windows, BLOCK), bf16),
            pltpu.VMEM((channels, rows, BLOCK), bf16),
            pltpu.VMEM((channels, rows, BLOCK), bf16),
            pltpu.VMEM((rounds, depth, BLOCK), bf16),
            pltpu.VMEM((rounds, 2, QUAD, rows, BLOCK), bf16),
            pltpu.VMEM((wide, wide), bf16),
            pltpu.VMEM((QUAD, pairs * 4 * windows, wide), bf16),
            pltpu.VMEM((TONES, 2, pairs * 2 * windows, wide), bf16),
            pltpu.VMEM((2, TONES, 2, wide // 2, pairs * 8 * windows), bf16),
            pltpu.VMEM((QUAD, rows, 2 * BLOCK), bf16),
            pltpu.VMEM((rounds, TONES, pairs * 8 * windows, 2 * BLOCK), bf16),
            pltpu.VMEM((2, TONES * 2 * channels, 2 * BLOCK), f32),
            pltpu.VMEM((2, *stack), f32),
            pltpu.VMEM((rounds, 2, *stack), bf16),
            pltpu.VMEM((rounds - 1, 2, *stack), bf16),
            pltpu.VMEM(stack, bf16),
            pltpu.VMEM(stack, bf16),
            pltpu.VMEM((per_round, channels, 2 * MAX_LAG + BLOCK), f32),
            dma((2, channels)),
            dma((rounds, 2)),
            dma((rounds, 2)),
            dma((rounds, QUAD)),
            dma((rounds, QUAD)),
            dma((rounds - 1, 2)),
            dma((rounds - 1, 2)),
            dma((2,)),
        ],
        compiler_params=pltpu.CompilerParams(
            vmem_limit_bytes=48 * 1024 * 1024, collective_id=1, has_side_effects=True
        ),
    )(pieces, sources, *tables)


def on_device(strain, sources):
    channels, windows, samples = strain.shape
    rounds, per_round = sources.shape
    total_sources = rounds * per_round
    factor = 1.0 / math.sqrt(lax.axis_size("win") * windows * samples)
    blocks = -(-samples // BLOCK)
    while blocks * windows % 16:
        blocks += 1
    depth = blocks * windows

    whitened = whiten(strain)
    padded = jnp.pad(whitened, ((0, 0), (0, 0), (0, blocks * BLOCK - samples)))
    pieces = padded.reshape(channels, windows, blocks, BLOCK)
    pieces = jnp.transpose(pieces, (0, 2, 1, 3)).reshape(channels, depth, BLOCK)

    if halves_fit(channels, windows, blocks, rounds, per_round):
        return correlate_halves(pieces, sources.astype(jnp.int32), factor)

    flat_sources = sources.reshape(-1)
    per_shard = total_sources // lax.axis_size("chan")
    owner = flat_sources // channels
    position = jnp.arange(total_sources)
    earlier = (owner[None, :] == owner[:, None]) & (position[None, :] < position[:, None])
    rank = jnp.sum(earlier.astype(jnp.int32), axis=1)
    me = lax.axis_index("chan")
    mine = owner == me
    slot_pick = (mine[None, :] & (rank[None, :] == jnp.arange(per_shard)[:, None])).astype(jnp.int32)
    local_channel = jnp.sum(slot_pick * (flat_sources - me * channels)[None, :], axis=1)
    order = (owner * per_shard + rank).astype(jnp.int32)

    return correlate(pieces, local_channel.astype(jnp.int32), order, windows, rounds, factor)


def solution(mesh):
    in_specs = (P("chan", "win", None), P())
    out_specs = P("win", "chan", None)
    return jax.shard_map(
        on_device, mesh=mesh, in_specs=in_specs, out_specs=out_specs, check_vma=False
    )
```

```python
import functools
import math

import jax
import jax.numpy as jnp
import ml_dtypes
import numpy as np
from jax import lax
from jax.experimental import pallas as pl
from jax.experimental.pallas import tpu as pltpu
from jax.sharding import PartitionSpec as P

MAX_LAG = 256
BLOCK = 128


def whiten(strain):
    mean_square = jnp.mean(strain * strain, axis=-1, keepdims=True)
    return (strain * lax.rsqrt(mean_square + 1e-06)).astype(jnp.bfloat16)


def ring_position(index, size):
    odd = lax.rem(index, 2)
    half = index // 2
    return (1 - odd) * half + odd * (size - 1 - half)


def ring_index(position, size):
    back = position // (size // 2)
    return (1 - back) * 2 * position + back * (2 * (size - 1 - position) + 1)


def kernel(
    sizes, streamed, factor, pieces_ref, local_ref, order_ref, out_ref,
    recv_ref, wide_ref, held_ref, own_ref, probe_ref, partial_ref, send_ref, land_ref,
    send_sem, recv_sem, stack_send_sem, stack_recv_sem,
):
    chan_size, win_size, lag_blocks, windows, front = sizes
    channels = recv_ref.shape[0]
    ways, _, count, depth, _ = held_ref.shape
    per_shard = ways * count
    here = ring_position(lax.axis_index("chan"), chan_size)
    win = lax.axis_index("win")
    right = ring_index(lax.rem(here + 1, chan_size), chan_size)
    left = ring_index(lax.rem(here + chan_size - 1, chan_size), chan_size)
    targets = [right, left]

    barrier = pltpu.get_barrier_semaphore()
    for chan in targets:
        pl.semaphore_signal(barrier, inc=1, device_id={"chan": chan}, device_id_type=pl.DeviceIdType.MESH)
    for step in range(1, win_size):
        peer = lax.rem(win + step, win_size)
        pl.semaphore_signal(barrier, inc=1, device_id={"win": peer}, device_id_type=pl.DeviceIdType.MESH)
    for way in range(ways):
        for item in range(count):
            held_ref[way, 0, item] = pieces_ref[local_ref[way * count + item]]
    own_ref[...] = jnp.zeros_like(own_ref)
    probe_ref[...] = jnp.zeros_like(probe_ref)
    pl.semaphore_wait(barrier, len(targets) + win_size - 1)

    row = lax.broadcasted_iota(jnp.int32, (BLOCK, BLOCK), 0)
    lane = lax.broadcasted_iota(jnp.int32, (BLOCK, BLOCK), 1)
    later = row + lane >= BLOCK - 1
    diagonal = row + lane == BLOCK - 1

    def hop(way, step, item):
        return pltpu.make_async_remote_copy(
            src_ref=held_ref.at[way, step, item],
            dst_ref=held_ref.at[way, step + 1, item],
            send_sem=send_sem.at[way, step, item],
            recv_sem=recv_sem.at[way, step, item],
            device_id={"chan": targets[way]},
            device_id_type=pl.DeviceIdType.MESH,
        )

    def stack_hop(dest, origin):
        slot = lax.rem(dest - win + win_size, win_size) - 1
        return pltpu.make_async_remote_copy(
            src_ref=partial_ref.at[origin * per_shard + dest],
            dst_ref=land_ref.at[slot, origin],
            send_sem=stack_send_sem.at[dest, origin],
            recv_sem=stack_recv_sem.at[slot, origin],
            device_id={"win": jnp.int32(dest)},
            device_id_type=pl.DeviceIdType.MESH,
        )

    def origin_of(way, step):
        position = here - step if way == 0 else here + step
        return ring_index(lax.rem(position + chan_size, chan_size), chan_size)

    def load(probe, item, step):
        for way in range(ways):
            probe[item, :depth, way * BLOCK : (way + 1) * BLOCK] = held_ref[way, step, item]

    def work(probe, item, step, channel):
        products = jnp.dot(recv_ref[channel], probe[item], preferred_element_type=jnp.float32)
        for way in range(ways):
            columns = products[:, way * BLOCK : (way + 1) * BLOCK]
            parts = [columns[k * BLOCK : (k + 1) * BLOCK] for k in range(lag_blocks + 1)]
            totals = []
            for k in range(lag_blocks):
                mixed = jnp.where(later, parts[k], parts[k + 1])
                sheared = pltpu.roll(mixed, 0, 1, stride=1, stride_axis=0)
                total = jnp.sum(sheared, axis=0, keepdims=True)
                totals.append(pltpu.roll(total, 1, 1) * factor)
            last = jnp.where(diagonal, parts[lag_blocks], 0.0)
            last = jnp.sum(jnp.sum(last, axis=0, keepdims=True), axis=1, keepdims=True)
            totals.append(jnp.broadcast_to(last * factor, (1, BLOCK)))
            place = origin_of(way, step) * per_shard + way * count + item
            partial_ref[place, pl.ds(channel, 1), :] = jnp.concatenate(totals, axis=1)

    def send_stacks(item, step):
        if not streamed:
            return
        for way in range(ways):
            dest = way * count + item

            @pl.when(win != dest)
            def _():
                stack_hop(dest, origin_of(way, step)).start()

    for way in range(ways):
        for item in range(count):
            hop(way, 0, item).start()

    reverse = jnp.where(diagonal, 1.0, 0.0).astype(jnp.bfloat16)
    inner = recv_ref.shape[2]
    reach = wide_ref.shape[1]
    wide_ref[...] = jnp.zeros_like(wide_ref)
    for channel in range(channels):
        wide_ref[channel % 2, front : front + depth, :] = pieces_ref[channel]
        flipped = lax.dot_general(
            reverse, wide_ref[channel % 2], (((1,), (1,)), ((), ())), preferred_element_type=jnp.float32
        )
        for k in range(lag_blocks + 1):
            shift = (lag_blocks - k) * windows
            moved = pltpu.roll(flipped, reach - shift, 1) if shift else flipped
            recv_ref[channel, k * BLOCK : (k + 1) * BLOCK, :] = moved[:, :inner].astype(jnp.bfloat16)

    spread = chan_size - 1 if chan_size - 1 <= channels else 0
    for item in range(count):
        load(own_ref, item, 0)
        for channel in range(channels - spread):
            work(own_ref, item, 0, channel)

    def body(step, carry):
        for item in range(count):
            for way in range(ways):
                hop(way, step - 1, item).wait_recv()

                @pl.when(step < chan_size - 1)
                def _():
                    hop(way, step, item).start()

            load(probe_ref, item, step)
            if spread:
                work(own_ref, item, 0, channels - spread + step - 1)
            for channel in range(channels):
                work(probe_ref, item, step, channel)
            send_stacks(item, step)
        return carry

    lax.fori_loop(1, chan_size, body, 0)
    for item in range(count):
        send_stacks(item, 0)
    for step in range(chan_size - 1):
        for way in range(ways):
            for item in range(count):
                hop(way, step, item).wait_send()

    per_win = out_ref.shape[0]
    if streamed:
        def arrived(index, carry):
            for slot in range(win_size - 1):
                peer = lax.rem(win + slot + 1, win_size)
                pltpu.make_async_remote_copy(
                    src_ref=partial_ref.at[index],
                    dst_ref=land_ref.at[slot, index],
                    send_sem=stack_send_sem.at[slot, index],
                    recv_sem=stack_recv_sem.at[slot, index],
                    device_id={"win": peer},
                    device_id_type=pl.DeviceIdType.MESH,
                ).wait_recv()
            return carry

        lax.fori_loop(0, chan_size, arrived, 0)
        for item in range(per_win):
            place = order_ref[win * per_win + item]
            owner = lax.div(place, per_shard)
            total = partial_ref[place]
            for slot in range(win_size - 1):
                total = total + land_ref[slot, owner]
            out_ref[item] = total[:, : out_ref.shape[2]]

        def sent(index, carry):
            for dest in range(win_size):
                @pl.when(win != dest)
                def _():
                    stack_hop(dest, index).wait_send()
            return carry

        lax.fori_loop(0, chan_size, sent, 0)
        return

    for dest in range(win_size):
        for item in range(per_win):
            send_ref[dest, item] = partial_ref[order_ref[dest * per_win + item]]

    def stack_copy(step):
        peer = lax.rem(win + step, win_size)
        return pltpu.make_async_remote_copy(
            src_ref=send_ref.at[peer],
            dst_ref=land_ref.at[step - 1],
            send_sem=stack_send_sem.at[step - 1],
            recv_sem=stack_recv_sem.at[step - 1],
            device_id={"win": peer},
            device_id_type=pl.DeviceIdType.MESH,
        )

    for step in range(1, win_size):
        stack_copy(step).start()
    for step in range(1, win_size):
        stack_copy(step).wait_recv()
    total = send_ref[win]
    for step in range(1, win_size):
        total = total + land_ref[step - 1]
    out_ref[...] = total[:, :, : out_ref.shape[2]]
    for step in range(1, win_size):
        stack_copy(step).wait_send()


def correlate(pieces, local_channel, order, windows, rounds, factor):
    channels, depth, _ = pieces.shape
    per_shard = local_channel.shape[0]
    total = order.shape[0]
    chan_size, win_size = lax.axis_size("chan"), lax.axis_size("win")
    lag_blocks = 2 * MAX_LAG // BLOCK
    lag_count = 2 * MAX_LAG + 1
    front = (lag_blocks - MAX_LAG // BLOCK) * windows
    inner = -(-depth // 256) * 256
    reach = -(-(inner + lag_blocks * windows) // BLOCK) * BLOCK
    lanes = (lag_blocks + 1) * BLOCK
    per_win = total // win_size
    streamed = rounds == win_size and total // rounds == chan_size and per_shard == rounds
    stack_copies = (win_size, chan_size) if streamed else (win_size - 1,)
    ways = 2 if per_shard % 2 == 0 else 1
    count = per_shard // ways
    return pl.pallas_call(
        functools.partial(kernel, (chan_size, win_size, lag_blocks, windows, front), streamed, factor),
        out_shape=jax.ShapeDtypeStruct((per_win, channels, lag_count), jnp.float32),
        in_specs=[
            pl.BlockSpec(memory_space=pltpu.VMEM),
            pl.BlockSpec(memory_space=pltpu.SMEM),
            pl.BlockSpec(memory_space=pltpu.SMEM),
        ],
        out_specs=pl.BlockSpec(memory_space=pltpu.VMEM),
        scratch_shapes=[
            pltpu.VMEM((channels, (lag_blocks + 1) * BLOCK, inner), jnp.bfloat16),
            pltpu.VMEM((2, reach, BLOCK), jnp.bfloat16),
            pltpu.VMEM((ways, chan_size, count, depth, BLOCK), jnp.bfloat16),
            pltpu.VMEM((count, inner, ways * BLOCK), jnp.bfloat16),
            pltpu.VMEM((count, inner, ways * BLOCK), jnp.bfloat16),
            pltpu.VMEM((total, channels, lanes), jnp.float32),
            pltpu.VMEM((win_size, per_win, channels, lanes), jnp.float32),
            pltpu.VMEM((win_size - 1, per_win, channels, lanes), jnp.float32),
            pltpu.SemaphoreType.DMA((ways, chan_size - 1, count)),
            pltpu.SemaphoreType.DMA((ways, chan_size - 1, count)),
            pltpu.SemaphoreType.DMA(stack_copies),
            pltpu.SemaphoreType.DMA(stack_copies),
        ],
        compiler_params=pltpu.CompilerParams(
            vmem_limit_bytes=48 * 1024 * 1024, collective_id=0, has_side_effects=True
        ),
    )(pieces, local_channel, order)


STEP = 32
QUAD = BLOCK // STEP
TAPS = MAX_LAG // STEP
POINTS = 3 * TAPS
TONES = POINTS // 2
LAGS = 2 * MAX_LAG // STEP + 1
HALO = MAX_LAG // BLOCK


def tones():
    return 2 * np.pi * (np.arange(TONES) + 0.5) / POINTS


def wave_rows():
    angle = np.outer(tones(), np.arange(POINTS))
    rows = np.stack([np.cos(angle), -np.sin(angle)], axis=1)
    scales = np.linspace(1.0, 2.0, 2000, endpoint=False)
    kept, used = [], []
    for row in rows:
        scaled = scales[:, None, None] * row
        near = scaled.astype(ml_dtypes.bfloat16).astype(np.float64)
        error = np.sum((near / scales[:, None, None] - row) ** 2, axis=(1, 2))
        best = int(np.argmin(error))
        kept.append(near[best])
        used.append(scales[best])
    return np.array(kept), np.array(used)


def constants(windows, channels, factor):
    rows, scales = wave_rows()
    bf16 = ml_dtypes.bfloat16
    perm = np.zeros((QUAD, QUAD, STEP, QUAD, STEP, QUAD), np.float32)
    for o in range(QUAD):
        for q in range(QUAD):
            perm[o, q, np.arange(STEP), q, np.arange(STEP), o] = 1
    perm = perm.reshape(QUAD * BLOCK, QUAD * BLOCK)
    parts = channels // QUAD
    turn = np.zeros((STEP, parts, QUAD, parts, STEP, QUAD), np.float32)
    for part in range(parts):
        for c in range(QUAD):
            turn[np.arange(STEP), part, c, part, np.arange(STEP), c] = 1
    turn = turn.reshape(STEP * channels, STEP * channels)
    eye = np.eye(windows)

    def dft(taps):
        blocks = (taps + TAPS) // QUAD
        out = np.zeros((TONES, 2, 2, windows, QUAD, blocks, windows))
        for seg in range(2):
            for n in range(taps):
                place = seg * TAPS + n
                out[:, :, seg, :, place % QUAD, place // QUAD, :] = rows[:, :, n, None, None] * eye
        return out.reshape(TONES * 4 * windows, QUAD * blocks * windows)

    phase = np.repeat(np.outer(tones(), np.arange(STEP) / STEP), QUAD, axis=1)
    twist = np.stack([np.cos(phase), np.sin(phase)], axis=1)
    twist = np.broadcast_to(twist[:, :, None, :], (TONES, 2, 8, BLOCK))
    angle = np.outer(np.arange(LAGS), tones())
    back = np.stack([np.cos(angle), -np.sin(angle)], axis=2) * (factor / TONES / scales**2)[:, None]
    inverse = np.einsum("kfv,cd->kcfvd", back, np.eye(channels)).reshape(LAGS * channels, TONES * 2 * channels)
    return (
        jnp.asarray(perm.astype(bf16)),
        jnp.asarray(turn.astype(bf16)),
        jnp.asarray(dft(TAPS).astype(bf16)),
        jnp.asarray(dft(POINTS).astype(bf16)),
        jnp.asarray(np.ascontiguousarray(twist).astype(np.float32)),
        jnp.asarray(inverse.astype(np.float32)),
    )


def halves_kernel(
    windows, pieces_ref, sources_ref, perm_ref, turn_ref, dft_a_ref, dft_b_ref, twist_ref, inverse_ref, out_ref,
    near_ref, pair_ref, own_ref, pick_ref, held_ref, spun_ref, xa_ref, sa_ref, a_ref, xb_ref, sb_ref, spec_ref, res_ref, sent_ref, land_ref,
    half_ref, part_ref, fin_ref,
    pair_sem, far_send, far_recv, side_send, side_recv, stack_send, stack_recv, end_sem,
):
    channels, depth, _ = pieces_ref.shape
    rounds, per_round = sources_ref.shape
    rows = held_ref.shape[3]
    halo = HALO * windows
    span = depth // 2
    size = span + halo
    pairs = sb_ref.shape[2] // 4 // (2 * windows)
    two = 2 * windows
    chan = lax.axis_index("chan")
    win = lax.axis_index("win")
    z, y = lax.div(chan, 2), lax.rem(chan, 2)
    half = lax.rem(z, 2)
    pair_z = z + 1 - 2 * half
    far = [lax.rem(z - half + 2 + k, QUAD) for k in range(2)]
    order = [z, pair_z] + far
    MESH = pl.DeviceIdType.MESH

    def source_rows(h):
        return pl.ds(pl.multiple_of(h * (span - halo), 16), size)

    def held_rows(h):
        return pl.ds(pl.multiple_of((1 - h) * halo, 16), size)

    def round_at(step):
        return lax.rem(win + jnp.where(step == 0, 2, jnp.where(step == 1, 1, jnp.where(step == 2, 3, 0))), rounds)

    def channel_of(step, shard):
        found = jnp.int32(0)
        for i in range(per_round):
            source = sources_ref[round_at(step), i]
            found += jnp.where(source // channels == shard, source - shard * channels, 0)
        return found

    def plan(shard):
        wanted = [channel_of(step, shard) for step in range(rounds)]
        first = []
        for step in range(rounds):
            found = jnp.int32(step)
            for earlier in reversed(range(step)):
                found = jnp.where(wanted[earlier] == wanted[step], earlier, found)
            first.append(found)
        ranks, free = [], jnp.int32(0)
        for c in range(channels):
            taken = jnp.int32(0)
            for channel in wanted:
                taken = jnp.where(channel == c, 1, taken)
            ranks.append(jnp.where(taken == 1, -1, free))
            free = free + 1 - taken
        line, spare = [], jnp.int32(0)
        for place in range(channels):
            filler = jnp.int32(0)
            for c in range(channels):
                filler = jnp.where(ranks[c] == spare, c, filler)
            if place < rounds:
                repeated = jnp.where(first[place] == place, 0, 1)
                line.append(jnp.where(repeated == 1, filler, wanted[place]))
                spare = spare + repeated
            else:
                line.append(filler)
                spare = spare + 1
        return wanted, first, line

    barrier = pltpu.get_barrier_semaphore()
    edge = jnp.zeros((16, BLOCK), jnp.bfloat16)
    edges = [*range(0, halo, 16), *range(size, rows, 16)]
    for at in edges:
        for step in range(rounds):
            for side in range(2):
                for zz in range(QUAD):
                    held_ref[step, side, zz, at : at + 16, :] = edge
        for c in range(channels):
            pair_ref[c, at : at + 16, :] = edge
            own_ref[c, at : at + 16, :] = edge
    peers = [{"chan": pair_z * 2 + y}, {"chan": far[0] * 2 + y}, {"chan": far[1] * 2 + y}, {"chan": z * 2 + 1 - y}]
    peers += [{"win": lax.rem(win + 1 + step, rounds)} for step in range(rounds - 1)]
    for peer in peers:
        pl.semaphore_signal(barrier, inc=1, device_id=peer, device_id_type=MESH)

    def near_copy(place):
        return pltpu.make_async_remote_copy(
            src_ref=near_ref.at[place],
            dst_ref=pair_ref.at[place, held_rows(1 - half), :],
            send_sem=pair_sem.at[0, place],
            recv_sem=pair_sem.at[1, place],
            device_id=peers[0],
            device_id_type=MESH,
        )

    def near_wait(place):
        pltpu.make_async_remote_copy(
            src_ref=near_ref.at[place],
            dst_ref=pair_ref.at[place, held_rows(half), :],
            send_sem=pair_sem.at[0, place],
            recv_sem=pair_sem.at[1, place],
            device_id=peers[0],
            device_id_type=MESH,
        ).wait_recv()

    def far_copy(step, k):
        return pltpu.make_async_remote_copy(
            src_ref=pick_ref.at[step, source_rows(k), :],
            dst_ref=held_ref.at[step, 0, z, held_rows(k), :],
            send_sem=far_send.at[step, k],
            recv_sem=far_recv.at[step, half],
            device_id=peers[1 + k],
            device_id_type=MESH,
        )

    def far_wait(step, k):
        pltpu.make_async_remote_copy(
            src_ref=pick_ref.at[step, source_rows(half), :],
            dst_ref=held_ref.at[step, 0, far[k], held_rows(half), :],
            send_sem=far_send.at[step, k],
            recv_sem=far_recv.at[step, k],
            device_id=peers[1 + k],
            device_id_type=MESH,
        ).wait_recv()

    def side_copy(step, o):
        return pltpu.make_async_remote_copy(
            src_ref=held_ref.at[step, 0, order[o], held_rows(half), :],
            dst_ref=held_ref.at[step, 1, order[o], held_rows(half), :],
            send_sem=side_send.at[step, o],
            recv_sem=side_recv.at[step, o],
            device_id=peers[3],
            device_id_type=MESH,
        )

    def stack_copy(step, which):
        return pltpu.make_async_remote_copy(
            src_ref=sent_ref.at[step, which],
            dst_ref=land_ref.at[step, which],
            send_sem=stack_send.at[step, which],
            recv_sem=stack_recv.at[step, which],
            device_id={"win": round_at(step)},
            device_id_type=MESH,
        )

    end_copy = pltpu.make_async_remote_copy(
        src_ref=half_ref,
        dst_ref=part_ref,
        send_sem=end_sem.at[0],
        recv_sem=end_sem.at[1],
        device_id=peers[0],
        device_id_type=MESH,
    )

    wanted, _, line = plan(chan)
    for step in range(rounds):
        pick_ref[step] = pieces_ref[wanted[step]]
        held_ref[step, 0, z, held_rows(half), :] = pick_ref[step, source_rows(half), :]
    for place in range(channels):
        near_ref[place] = pieces_ref[line[place], source_rows(1 - half), :]
    pl.semaphore_wait(barrier, len(peers))
    ahead = [1, 2, 5, 8]
    sent = 0
    for step in range(rounds):
        for place in range(sent, ahead[step]):
            near_copy(place).start()
        sent = ahead[step]
        for k in range(2):
            far_copy(step, k).start()
    for step in range(rounds):
        side_copy(step, 0).start()
    for c in range(channels):
        own_ref[c, held_rows(half), :] = pieces_ref[c, source_rows(half), :]

    def twisted(real, imag, f):
        cos, sin = twist_ref[f, 0], twist_ref[f, 1]
        reals, imags = [], []
        for part in range(real.shape[1] // BLOCK):
            lanes = slice(part * BLOCK, (part + 1) * BLOCK)
            turned = []
            for at in range(0, real.shape[0], 8):
                re, im = real[at : at + 8, lanes], imag[at : at + 8, lanes]
                turned.append((re * cos + im * sin, im * cos - re * sin))
            reals.append(jnp.concatenate([t[0] for t in turned], axis=0))
            imags.append(jnp.concatenate([t[1] for t in turned], axis=0))
        return jnp.concatenate(reals, axis=1).astype(jnp.bfloat16), jnp.concatenate(imags, axis=1).astype(jnp.bfloat16)

    def half_turn(value):
        return pltpu.roll(value, BLOCK // 2, 1)

    def spread(refs, at, count, put):
        joined = jnp.concatenate([r[at : at + count, :] for r in refs], axis=1)
        put(jnp.dot(joined, perm_ref[...], preferred_element_type=jnp.float32).astype(jnp.bfloat16))

    def receivers(which, ref, spin_ref):
        for part in range(channels // QUAD):
            def put(value):
                for q in range(QUAD):
                    xa_ref[q, 0:span, part * BLOCK : (part + 1) * BLOCK] = value[:, q * BLOCK : (q + 1) * BLOCK]

            spread([ref.at[part * QUAD + o] for o in range(QUAD)], halo, span, put)

        def waves(g, carry):
            at = pl.multiple_of(g * two * TAPS // QUAD, 16)
            taken = jnp.concatenate([xa_ref[q, pl.ds(at, two * TAPS // QUAD), :] for q in range(QUAD)], axis=0)
            seen = jnp.dot(dft_a_ref[...], taken, preferred_element_type=jnp.float32)
            here = pl.multiple_of(g * two, 16)
            for f in range(TONES):
                real, imag = twisted(seen[2 * f * two : (2 * f + 1) * two], seen[(2 * f + 1) * two : (2 * f + 2) * two], f)
                sa_ref[f, 0, pl.ds(here, two), :] = real
                sa_ref[f, 1, pl.ds(here, two), :] = imag
            return carry

        lax.fori_loop(0, pairs, waves, 0, unroll=8)
        wide = pairs * two

        def turned(f, carry):
            real, imag = [
                lax.dot_general(
                    spin_ref[...], sa_ref[f, v], (((1,), (1,)), ((), ())), preferred_element_type=jnp.float32
                ).astype(jnp.bfloat16)
                for v in range(2)
            ]
            deep = STEP * channels // 2
            for u in range(2):
                at = 2 * u * wide
                re, im = real[u * deep : (u + 1) * deep], imag[u * deep : (u + 1) * deep]
                a_ref[which, f, 0, :, at : at + wide] = re
                a_ref[which, f, 0, :, at + wide : at + 2 * wide] = im
                a_ref[which, f, 1, :, at : at + wide] = -im
                a_ref[which, f, 1, :, at + wide : at + 2 * wide] = re
            return carry

        lax.fori_loop(0, TONES, turned, 0, unroll=12)

    def sources(step):
        wide = pairs * two
        for side in range(2):
            def put(value):
                for q in range(QUAD):
                    xb_ref[q, :, side * BLOCK : (side + 1) * BLOCK] = value[:, q * BLOCK : (q + 1) * BLOCK]

            spread([held_ref.at[step, side, zz] for zz in range(QUAD)], 0, rows, put)

        def waves(g, carry):
            count = windows * (TAPS + POINTS) // QUAD
            at = pl.multiple_of(g * two * TAPS // QUAD, 16)
            taken = jnp.concatenate([xb_ref[q, pl.ds(at, count), :] for q in range(QUAD)], axis=0)
            seen = jnp.dot(dft_b_ref[...], taken, preferred_element_type=jnp.float32)
            here = pl.multiple_of(g * two, 16)
            for f in range(TONES):
                real, imag = twisted(seen[2 * f * two : (2 * f + 1) * two], seen[(2 * f + 1) * two : (2 * f + 2) * two], f)
                for v, part in enumerate((real, imag)):
                    sb_ref[step, f, pl.ds(pl.multiple_of(here + v * wide, 16), two), :] = part
                    for side in range(2):
                        lanes = slice(side * BLOCK, (side + 1) * BLOCK)
                        sb_ref[step, f, pl.ds(pl.multiple_of(here + (v + 2) * wide, 16), two), lanes] = half_turn(part[:, lanes])
            return carry

        lax.fori_loop(0, pairs, waves, 0, unroll=8)

    def products(step, which):
        def tone(f, carry):
            right = sb_ref[step, f]
            sums = []
            for v in range(2):
                seen = jnp.dot(a_ref[which, f, v], right, preferred_element_type=jnp.float32)
                for side in range(2):
                    lanes = slice(side * BLOCK, (side + 1) * BLOCK)
                    total = [None] * 4
                    for i in range(STEP // 2):
                        term = seen[i * channels : (i + 1) * channels, lanes]
                        if i:
                            term = pltpu.roll(term, BLOCK - QUAD * i, 1)
                        total[i % 4] = term if total[i % 4] is None else total[i % 4] + term
                    sums.append((total[0] + total[1]) + (total[2] + total[3]))
            cos, sin = twist_ref[f, 0], twist_ref[f, 1]
            at = pl.multiple_of(f * 2 * channels, 16)
            for side in range(2):
                lanes = slice(side * BLOCK, (side + 1) * BLOCK)
                re, im = sums[side], sums[2 + side]
                both = jnp.concatenate([re * cos - im * sin, re * sin + im * cos], axis=0)
                spec_ref[which, pl.ds(at, 2 * channels), lanes] = both
            return carry

        lax.fori_loop(0, TONES, tone, 0, unroll=12)
        sums = jnp.dot(
            inverse_ref[...], spec_ref[which], precision=lax.Precision.HIGHEST, preferred_element_type=jnp.float32
        )
        sums = jnp.concatenate([sums[:, :BLOCK], sums[:, BLOCK:]], axis=0)
        res_ref[which] = sums
        sent_ref[step, which] = sums.astype(jnp.bfloat16)

    _, first, pair_line = plan(pair_z * 2 + y)

    def pass_on(step):
        if step < 3:
            near_wait(step)
        total = pair_ref[0, held_rows(half), :]
        if step:
            total = jnp.zeros(total.shape, jnp.float32)
            for place in range(step + 1):
                share = jnp.where(first[step] == place, 1.0, 0.0)
                total = total + pair_ref[place, held_rows(half), :].astype(jnp.float32) * share
            total = total.astype(jnp.bfloat16)
        held_ref[step, 0, pair_z, held_rows(half), :] = total
        side_copy(step, 1).start()
        for k in range(2):
            far_wait(step, k)
            side_copy(step, 2 + k).start()

    def take(step):
        for o in range(QUAD):
            side_copy(step, o).wait_recv()
        sources(step)

    xa_ref[:, span:, :] = jnp.zeros((QUAD, xa_ref.shape[1] - span, xa_ref.shape[2]), jnp.bfloat16)
    receivers(0, own_ref, turn_ref)
    row = lax.broadcasted_iota(jnp.int32, spun_ref.shape, 0)
    lane = lax.broadcasted_iota(jnp.int32, spun_ref.shape, 1)
    place = lane // BLOCK * QUAD + lane % QUAD
    meant = jnp.zeros_like(lane)
    for c in range(channels):
        meant = jnp.where(place == c, pair_line[c], meant)
    hit = (lane % BLOCK // QUAD * channels + meant) == row
    spun_ref[...] = jnp.where(hit, 1.0, 0.0).astype(jnp.bfloat16)
    pass_on(0)
    pass_on(1)

    def early(step, carry):
        take(step)
        products(step, 0)
        stack_copy(step, 0).start()

        @pl.when(step == 0)
        def _():
            pass_on(2)

        return carry

    lax.fori_loop(0, 2, early, 0)
    for place in range(3, channels):
        near_wait(place)
    receivers(1, pair_ref, spun_ref)

    def shared(step, carry):
        products(step, 1)
        stack_copy(step, 1).start()

        @pl.when(step == 0)
        def _():
            pass_on(3)

        return carry

    lax.fori_loop(0, 2, shared, 0)

    def summed(which):
        total = res_ref[which]
        for step in range(rounds - 1):
            stack_copy(step, which).wait_recv()
            total = total + land_ref[step, which].astype(jnp.float32)
        return total

    def late(step, carry):
        take(step)

        def each(index, carry):
            products(step, 1 - index)

            @pl.when(step < rounds - 1)
            def _():
                stack_copy(step, 1 - index).start()

            @pl.when((step == rounds - 1) & (index == 0))
            def _():
                half_ref[...] = summed(1).astype(jnp.bfloat16)
                end_copy.start()

            return carry

        lax.fori_loop(0, 2, each, 0)
        return carry

    lax.fori_loop(2, rounds, late, 0)
    whole_sum = summed(0)
    for step in range(rounds):
        for k in range(2):
            far_copy(step, k).wait_send()
        for o in range(QUAD):
            side_copy(step, o).wait_send()
    for place in range(channels):
        near_copy(place).wait_send()
    for step in range(rounds - 1):
        for which in range(2):
            stack_copy(step, which).wait_send()
    end_copy.wait_recv()
    both = whole_sum + part_ref[...].astype(jnp.float32)
    groups = (LAGS - 1) // QUAD
    for side in range(2):
        total = both[side * LAGS * channels : (side + 1) * LAGS * channels]
        lined = jnp.concatenate(
            [
                jnp.concatenate(
                    [total[(QUAD * g + q) * channels : (QUAD * g + q + 1) * channels] for g in range(groups)], axis=0
                )
                for q in range(QUAD)
            ],
            axis=1,
        )
        high = lined.astype(jnp.bfloat16)
        rest = lined - high.astype(jnp.float32)
        middle = rest.astype(jnp.bfloat16)
        low = (rest - middle.astype(jnp.float32)).astype(jnp.bfloat16)
        split = [
            lax.dot_general(p, perm_ref[...], (((1,), (1,)), ((), ())), preferred_element_type=jnp.float32)
            for p in (high, middle, low)
        ]
        whole = split[0] + split[1] + split[2]
        last = total[(LAGS - 1) * channels : LAGS * channels]
        for zz in range(QUAD):
            for g in range(groups):
                fin_ref[side * QUAD + zz, :, g * BLOCK : (g + 1) * BLOCK] = whole[
                    g * channels : (g + 1) * channels, zz * BLOCK : (zz + 1) * BLOCK
                ]
            fin_ref[side * QUAD + zz, :, groups * BLOCK : (groups + 1) * BLOCK] = jnp.broadcast_to(
                last[:, zz : zz + 1], (channels, BLOCK)
            )
    for i in range(per_round):
        shard = sources_ref[win, i] // channels
        side = jnp.where(shard - 2 * (shard // 2) == y, 0, 1)
        out_ref[i] = fin_ref[side * QUAD + shard // 2][:, : out_ref.shape[2]]
    end_copy.wait_send()


def halves_fit(channels, windows, blocks, rounds, per_round):
    chan_size, win_size = lax.axis_size("chan"), lax.axis_size("win")
    return (
        rounds == win_size
        and per_round == chan_size
        and chan_size == 2 * QUAD
        and win_size == QUAD
        and channels == 2 * QUAD
        and windows == 8
        and blocks % 4 == 0
    )


def correlate_halves(pieces, sources, factor):
    channels, depth, _ = pieces.shape
    rounds, per_round = sources.shape
    windows = 8
    tables = constants(windows, channels, factor)
    span = depth // 2
    pairs = -(-span // (windows * 4))
    rows = (pairs * 4 + 2 * HALO) * windows
    wide = channels * STEP
    stack = (2 * LAGS * channels, BLOCK)
    bf16, f32 = jnp.bfloat16, jnp.float32
    dma = pltpu.SemaphoreType.DMA
    return pl.pallas_call(
        functools.partial(halves_kernel, windows),
        out_shape=jax.ShapeDtypeStruct((per_round, channels, 2 * MAX_LAG + 1), f32),
        in_specs=[pl.BlockSpec(memory_space=pltpu.VMEM), pl.BlockSpec(memory_space=pltpu.SMEM)]
        + [pl.BlockSpec(memory_space=pltpu.VMEM)] * len(tables),
        out_specs=pl.BlockSpec(memory_space=pltpu.VMEM),
        scratch_shapes=[
            pltpu.VMEM((channels, span + HALO * windows, BLOCK), bf16),
            pltpu.VMEM((channels, rows, BLOCK), bf16),
            pltpu.VMEM((channels, rows, BLOCK), bf16),
            pltpu.VMEM((rounds, depth, BLOCK), bf16),
            pltpu.VMEM((rounds, 2, QUAD, rows, BLOCK), bf16),
            pltpu.VMEM((wide, wide), bf16),
            pltpu.VMEM((QUAD, pairs * 4 * windows, wide), bf16),
            pltpu.VMEM((TONES, 2, pairs * 2 * windows, wide), bf16),
            pltpu.VMEM((2, TONES, 2, wide // 2, pairs * 8 * windows), bf16),
            pltpu.VMEM((QUAD, rows, 2 * BLOCK), bf16),
            pltpu.VMEM((rounds, TONES, pairs * 8 * windows, 2 * BLOCK), bf16),
            pltpu.VMEM((2, TONES * 2 * channels, 2 * BLOCK), f32),
            pltpu.VMEM((2, *stack), f32),
            pltpu.VMEM((rounds, 2, *stack), bf16),
            pltpu.VMEM((rounds - 1, 2, *stack), bf16),
            pltpu.VMEM(stack, bf16),
            pltpu.VMEM(stack, bf16),
            pltpu.VMEM((per_round, channels, 2 * MAX_LAG + BLOCK), f32),
            dma((2, channels)),
            dma((rounds, 2)),
            dma((rounds, 2)),
            dma((rounds, QUAD)),
            dma((rounds, QUAD)),
            dma((rounds - 1, 2)),
            dma((rounds - 1, 2)),
            dma((2,)),
        ],
        compiler_params=pltpu.CompilerParams(
            vmem_limit_bytes=48 * 1024 * 1024, collective_id=1, has_side_effects=True
        ),
    )(pieces, sources, *tables)


def on_device(strain, sources):
    channels, windows, samples = strain.shape
    rounds, per_round = sources.shape
    total_sources = rounds * per_round
    factor = 1.0 / math.sqrt(lax.axis_size("win") * windows * samples)
    blocks = -(-samples // BLOCK)
    while blocks * windows % 16:
        blocks += 1
    depth = blocks * windows

    whitened = whiten(strain)
    padded = jnp.pad(whitened, ((0, 0), (0, 0), (0, blocks * BLOCK - samples)))
    pieces = padded.reshape(channels, windows, blocks, BLOCK)
    pieces = jnp.transpose(pieces, (0, 2, 1, 3)).reshape(channels, depth, BLOCK)

    if halves_fit(channels, windows, blocks, rounds, per_round):
        return correlate_halves(pieces, sources.astype(jnp.int32), factor)

    flat_sources = sources.reshape(-1)
    per_shard = total_sources // lax.axis_size("chan")
    owner = flat_sources // channels
    position = jnp.arange(total_sources)
    earlier = (owner[None, :] == owner[:, None]) & (position[None, :] < position[:, None])
    rank = jnp.sum(earlier.astype(jnp.int32), axis=1)
    me = lax.axis_index("chan")
    mine = owner == me
    slot_pick = (mine[None, :] & (rank[None, :] == jnp.arange(per_shard)[:, None])).astype(jnp.int32)
    local_channel = jnp.sum(slot_pick * (flat_sources - me * channels)[None, :], axis=1)
    order = (owner * per_shard + rank).astype(jnp.int32)

    return correlate(pieces, local_channel.astype(jnp.int32), order, windows, rounds, factor)


def solution(mesh):
    in_specs = (P("chan", "win", None), P())
    out_specs = P("win", "chan", None)
    return jax.shard_map(
        on_device, mesh=mesh, in_specs=in_specs, out_specs=out_specs, check_vma=False
    )
```

```python
import functools
import math

import jax
import jax.numpy as jnp
import ml_dtypes
import numpy as np
from jax import lax
from jax.experimental import pallas as pl
from jax.experimental.pallas import tpu as pltpu
from jax.sharding import PartitionSpec as P

MAX_LAG = 256
BLOCK = 128


def whiten(strain):
    mean_square = jnp.mean(strain * strain, axis=-1, keepdims=True)
    return (strain * lax.rsqrt(mean_square + 1e-06)).astype(jnp.bfloat16)


def ring_position(index, size):
    odd = lax.rem(index, 2)
    half = index // 2
    return (1 - odd) * half + odd * (size - 1 - half)


def ring_index(position, size):
    back = position // (size // 2)
    return (1 - back) * 2 * position + back * (2 * (size - 1 - position) + 1)


def kernel(
    sizes, streamed, factor, pieces_ref, local_ref, order_ref, out_ref,
    recv_ref, wide_ref, held_ref, own_ref, probe_ref, partial_ref, send_ref, land_ref,
    send_sem, recv_sem, stack_send_sem, stack_recv_sem,
):
    chan_size, win_size, lag_blocks, windows, front = sizes
    channels = recv_ref.shape[0]
    ways, _, count, depth, _ = held_ref.shape
    per_shard = ways * count
    here = ring_position(lax.axis_index("chan"), chan_size)
    win = lax.axis_index("win")
    right = ring_index(lax.rem(here + 1, chan_size), chan_size)
    left = ring_index(lax.rem(here + chan_size - 1, chan_size), chan_size)
    targets = [right, left]

    barrier = pltpu.get_barrier_semaphore()
    for chan in targets:
        pl.semaphore_signal(barrier, inc=1, device_id={"chan": chan}, device_id_type=pl.DeviceIdType.MESH)
    for step in range(1, win_size):
        peer = lax.rem(win + step, win_size)
        pl.semaphore_signal(barrier, inc=1, device_id={"win": peer}, device_id_type=pl.DeviceIdType.MESH)
    for way in range(ways):
        for item in range(count):
            held_ref[way, 0, item] = pieces_ref[local_ref[way * count + item]]
    own_ref[...] = jnp.zeros_like(own_ref)
    probe_ref[...] = jnp.zeros_like(probe_ref)
    pl.semaphore_wait(barrier, len(targets) + win_size - 1)

    row = lax.broadcasted_iota(jnp.int32, (BLOCK, BLOCK), 0)
    lane = lax.broadcasted_iota(jnp.int32, (BLOCK, BLOCK), 1)
    later = row + lane >= BLOCK - 1
    diagonal = row + lane == BLOCK - 1

    def hop(way, step, item):
        return pltpu.make_async_remote_copy(
            src_ref=held_ref.at[way, step, item],
            dst_ref=held_ref.at[way, step + 1, item],
            send_sem=send_sem.at[way, step, item],
            recv_sem=recv_sem.at[way, step, item],
            device_id={"chan": targets[way]},
            device_id_type=pl.DeviceIdType.MESH,
        )

    def stack_hop(dest, origin):
        slot = lax.rem(dest - win + win_size, win_size) - 1
        return pltpu.make_async_remote_copy(
            src_ref=partial_ref.at[origin * per_shard + dest],
            dst_ref=land_ref.at[slot, origin],
            send_sem=stack_send_sem.at[dest, origin],
            recv_sem=stack_recv_sem.at[slot, origin],
            device_id={"win": jnp.int32(dest)},
            device_id_type=pl.DeviceIdType.MESH,
        )

    def origin_of(way, step):
        position = here - step if way == 0 else here + step
        return ring_index(lax.rem(position + chan_size, chan_size), chan_size)

    def load(probe, item, step):
        for way in range(ways):
            probe[item, :depth, way * BLOCK : (way + 1) * BLOCK] = held_ref[way, step, item]

    def work(probe, item, step, channel):
        products = jnp.dot(recv_ref[channel], probe[item], preferred_element_type=jnp.float32)
        for way in range(ways):
            columns = products[:, way * BLOCK : (way + 1) * BLOCK]
            parts = [columns[k * BLOCK : (k + 1) * BLOCK] for k in range(lag_blocks + 1)]
            totals = []
            for k in range(lag_blocks):
                mixed = jnp.where(later, parts[k], parts[k + 1])
                sheared = pltpu.roll(mixed, 0, 1, stride=1, stride_axis=0)
                total = jnp.sum(sheared, axis=0, keepdims=True)
                totals.append(pltpu.roll(total, 1, 1) * factor)
            last = jnp.where(diagonal, parts[lag_blocks], 0.0)
            last = jnp.sum(jnp.sum(last, axis=0, keepdims=True), axis=1, keepdims=True)
            totals.append(jnp.broadcast_to(last * factor, (1, BLOCK)))
            place = origin_of(way, step) * per_shard + way * count + item
            partial_ref[place, pl.ds(channel, 1), :] = jnp.concatenate(totals, axis=1)

    def send_stacks(item, step):
        if not streamed:
            return
        for way in range(ways):
            dest = way * count + item

            @pl.when(win != dest)
            def _():
                stack_hop(dest, origin_of(way, step)).start()

    for way in range(ways):
        for item in range(count):
            hop(way, 0, item).start()

    reverse = jnp.where(diagonal, 1.0, 0.0).astype(jnp.bfloat16)
    inner = recv_ref.shape[2]
    reach = wide_ref.shape[1]
    wide_ref[...] = jnp.zeros_like(wide_ref)
    for channel in range(channels):
        wide_ref[channel % 2, front : front + depth, :] = pieces_ref[channel]
        flipped = lax.dot_general(
            reverse, wide_ref[channel % 2], (((1,), (1,)), ((), ())), preferred_element_type=jnp.float32
        )
        for k in range(lag_blocks + 1):
            shift = (lag_blocks - k) * windows
            moved = pltpu.roll(flipped, reach - shift, 1) if shift else flipped
            recv_ref[channel, k * BLOCK : (k + 1) * BLOCK, :] = moved[:, :inner].astype(jnp.bfloat16)

    spread = chan_size - 1 if chan_size - 1 <= channels else 0
    for item in range(count):
        load(own_ref, item, 0)
        for channel in range(channels - spread):
            work(own_ref, item, 0, channel)

    def body(step, carry):
        for item in range(count):
            for way in range(ways):
                hop(way, step - 1, item).wait_recv()

                @pl.when(step < chan_size - 1)
                def _():
                    hop(way, step, item).start()

            load(probe_ref, item, step)
            if spread:
                work(own_ref, item, 0, channels - spread + step - 1)
            for channel in range(channels):
                work(probe_ref, item, step, channel)
            send_stacks(item, step)
        return carry

    lax.fori_loop(1, chan_size, body, 0)
    for item in range(count):
        send_stacks(item, 0)
    for step in range(chan_size - 1):
        for way in range(ways):
            for item in range(count):
                hop(way, step, item).wait_send()

    per_win = out_ref.shape[0]
    if streamed:
        def arrived(index, carry):
            for slot in range(win_size - 1):
                peer = lax.rem(win + slot + 1, win_size)
                pltpu.make_async_remote_copy(
                    src_ref=partial_ref.at[index],
                    dst_ref=land_ref.at[slot, index],
                    send_sem=stack_send_sem.at[slot, index],
                    recv_sem=stack_recv_sem.at[slot, index],
                    device_id={"win": peer},
                    device_id_type=pl.DeviceIdType.MESH,
                ).wait_recv()
            return carry

        lax.fori_loop(0, chan_size, arrived, 0)
        for item in range(per_win):
            place = order_ref[win * per_win + item]
            owner = lax.div(place, per_shard)
            total = partial_ref[place]
            for slot in range(win_size - 1):
                total = total + land_ref[slot, owner]
            out_ref[item] = total[:, : out_ref.shape[2]]

        def sent(index, carry):
            for dest in range(win_size):
                @pl.when(win != dest)
                def _():
                    stack_hop(dest, index).wait_send()
            return carry

        lax.fori_loop(0, chan_size, sent, 0)
        return

    for dest in range(win_size):
        for item in range(per_win):
            send_ref[dest, item] = partial_ref[order_ref[dest * per_win + item]]

    def stack_copy(step):
        peer = lax.rem(win + step, win_size)
        return pltpu.make_async_remote_copy(
            src_ref=send_ref.at[peer],
            dst_ref=land_ref.at[step - 1],
            send_sem=stack_send_sem.at[step - 1],
            recv_sem=stack_recv_sem.at[step - 1],
            device_id={"win": peer},
            device_id_type=pl.DeviceIdType.MESH,
        )

    for step in range(1, win_size):
        stack_copy(step).start()
    for step in range(1, win_size):
        stack_copy(step).wait_recv()
    total = send_ref[win]
    for step in range(1, win_size):
        total = total + land_ref[step - 1]
    out_ref[...] = total[:, :, : out_ref.shape[2]]
    for step in range(1, win_size):
        stack_copy(step).wait_send()


def correlate(pieces, local_channel, order, windows, rounds, factor):
    channels, depth, _ = pieces.shape
    per_shard = local_channel.shape[0]
    total = order.shape[0]
    chan_size, win_size = lax.axis_size("chan"), lax.axis_size("win")
    lag_blocks = 2 * MAX_LAG // BLOCK
    lag_count = 2 * MAX_LAG + 1
    front = (lag_blocks - MAX_LAG // BLOCK) * windows
    inner = -(-depth // 256) * 256
    reach = -(-(inner + lag_blocks * windows) // BLOCK) * BLOCK
    lanes = (lag_blocks + 1) * BLOCK
    per_win = total // win_size
    streamed = rounds == win_size and total // rounds == chan_size and per_shard == rounds
    stack_copies = (win_size, chan_size) if streamed else (win_size - 1,)
    ways = 2 if per_shard % 2 == 0 else 1
    count = per_shard // ways
    return pl.pallas_call(
        functools.partial(kernel, (chan_size, win_size, lag_blocks, windows, front), streamed, factor),
        out_shape=jax.ShapeDtypeStruct((per_win, channels, lag_count), jnp.float32),
        in_specs=[
            pl.BlockSpec(memory_space=pltpu.VMEM),
            pl.BlockSpec(memory_space=pltpu.SMEM),
            pl.BlockSpec(memory_space=pltpu.SMEM),
        ],
        out_specs=pl.BlockSpec(memory_space=pltpu.VMEM),
        scratch_shapes=[
            pltpu.VMEM((channels, (lag_blocks + 1) * BLOCK, inner), jnp.bfloat16),
            pltpu.VMEM((2, reach, BLOCK), jnp.bfloat16),
            pltpu.VMEM((ways, chan_size, count, depth, BLOCK), jnp.bfloat16),
            pltpu.VMEM((count, inner, ways * BLOCK), jnp.bfloat16),
            pltpu.VMEM((count, inner, ways * BLOCK), jnp.bfloat16),
            pltpu.VMEM((total, channels, lanes), jnp.float32),
            pltpu.VMEM((win_size, per_win, channels, lanes), jnp.float32),
            pltpu.VMEM((win_size - 1, per_win, channels, lanes), jnp.float32),
            pltpu.SemaphoreType.DMA((ways, chan_size - 1, count)),
            pltpu.SemaphoreType.DMA((ways, chan_size - 1, count)),
            pltpu.SemaphoreType.DMA(stack_copies),
            pltpu.SemaphoreType.DMA(stack_copies),
        ],
        compiler_params=pltpu.CompilerParams(
            vmem_limit_bytes=48 * 1024 * 1024, collective_id=0, has_side_effects=True
        ),
    )(pieces, local_channel, order)


STEP = 32
QUAD = BLOCK // STEP
TAPS = MAX_LAG // STEP
POINTS = 3 * TAPS
TONES = POINTS // 2
LAGS = 2 * MAX_LAG // STEP + 1
HALO = MAX_LAG // BLOCK


def tones():
    return 2 * np.pi * (np.arange(TONES) + 0.5) / POINTS


def wave_rows():
    angle = np.outer(tones(), np.arange(POINTS))
    rows = np.stack([np.cos(angle), -np.sin(angle)], axis=1)
    scales = np.linspace(1.0, 2.0, 2000, endpoint=False)
    kept, used = [], []
    for row in rows:
        scaled = scales[:, None, None] * row
        near = scaled.astype(ml_dtypes.bfloat16).astype(np.float64)
        error = np.sum((near / scales[:, None, None] - row) ** 2, axis=(1, 2))
        best = int(np.argmin(error))
        kept.append(near[best])
        used.append(scales[best])
    return np.array(kept), np.array(used)


def constants(windows, channels, factor):
    rows, scales = wave_rows()
    bf16 = ml_dtypes.bfloat16
    perm = np.zeros((QUAD, QUAD, STEP, QUAD, STEP, QUAD), np.float32)
    for o in range(QUAD):
        for q in range(QUAD):
            perm[o, q, np.arange(STEP), q, np.arange(STEP), o] = 1
    perm = perm.reshape(QUAD * BLOCK, QUAD * BLOCK)
    parts = channels // QUAD
    turn = np.zeros((STEP, parts, QUAD, parts, STEP, QUAD), np.float32)
    for part in range(parts):
        for c in range(QUAD):
            turn[np.arange(STEP), part, c, part, np.arange(STEP), c] = 1
    turn = turn.reshape(STEP * channels, STEP * channels)
    eye = np.eye(windows)

    def dft(taps):
        blocks = (taps + TAPS) // QUAD
        out = np.zeros((TONES, 2, 2, windows, QUAD, blocks, windows))
        for seg in range(2):
            for n in range(taps):
                place = seg * TAPS + n
                out[:, :, seg, :, place % QUAD, place // QUAD, :] = rows[:, :, n, None, None] * eye
        return out.reshape(TONES * 4 * windows, QUAD * blocks * windows)

    phase = np.repeat(np.outer(tones(), np.arange(STEP) / STEP), QUAD, axis=1)
    twist = np.stack([np.cos(phase), np.sin(phase)], axis=1)
    twist = np.broadcast_to(twist[:, :, None, :], (TONES, 2, 8, BLOCK))
    angle = np.outer(np.arange(LAGS), tones())
    back = np.stack([np.cos(angle), -np.sin(angle)], axis=2) * (factor / TONES / scales**2)[:, None]
    inverse = np.einsum("kfv,cd->kcfvd", back, np.eye(channels)).reshape(LAGS * channels, TONES * 2 * channels)
    inverse = np.pad(inverse, ((0, -inverse.shape[0] % 16), (0, 0)))
    upper = inverse.astype(bf16)
    return (
        jnp.asarray(perm.astype(bf16)),
        jnp.asarray(turn.astype(bf16)),
        jnp.asarray(dft(TAPS).astype(bf16)),
        jnp.asarray(dft(POINTS).astype(bf16)),
        jnp.asarray(np.ascontiguousarray(twist).astype(np.float32)),
        jnp.asarray(np.concatenate([upper, (inverse - upper.astype(np.float64)).astype(bf16)], axis=0)),
    )


def halves_kernel(
    windows, pieces_ref, sources_ref, perm_ref, turn_ref, dft_a_ref, dft_b_ref, twist_ref, inverse_ref, out_ref,
    near_ref, pair_ref, own_ref, pick_ref, held_ref, spun_ref, xa_ref, sa_ref, a_ref, xb_ref, sb_ref, spec_ref, res_ref, sent_ref, land_ref,
    half_ref, part_ref, fin_ref,
    pair_sem, far_send, far_recv, side_send, side_recv, stack_send, stack_recv, end_sem,
):
    channels, depth, _ = pieces_ref.shape
    rounds, per_round = sources_ref.shape
    rows = held_ref.shape[3]
    halo = HALO * windows
    span = depth // 2
    size = span + halo
    pairs = sb_ref.shape[2] // 4 // (2 * windows)
    two = 2 * windows
    chan = lax.axis_index("chan")
    win = lax.axis_index("win")
    z, y = lax.div(chan, 2), lax.rem(chan, 2)
    half = lax.rem(z, 2)
    pair_z = z + 1 - 2 * half
    far = [lax.rem(z - half + 2 + k, QUAD) for k in range(2)]
    order = [z, pair_z] + far
    MESH = pl.DeviceIdType.MESH

    def source_rows(h):
        return pl.ds(pl.multiple_of(h * (span - halo), 16), size)

    def held_rows(h):
        return pl.ds(pl.multiple_of((1 - h) * halo, 16), size)

    def round_at(step):
        return lax.rem(win + jnp.where(step == 0, 2, jnp.where(step == 1, 1, jnp.where(step == 2, 3, 0))), rounds)

    def channel_of(step, shard):
        found = jnp.int32(0)
        for i in range(per_round):
            source = sources_ref[round_at(step), i]
            found += jnp.where(source // channels == shard, source - shard * channels, 0)
        return found

    def plan(shard):
        wanted = [channel_of(step, shard) for step in range(rounds)]
        first = []
        for step in range(rounds):
            found = jnp.int32(step)
            for earlier in reversed(range(step)):
                found = jnp.where(wanted[earlier] == wanted[step], earlier, found)
            first.append(found)
        ranks, free = [], jnp.int32(0)
        for c in range(channels):
            taken = jnp.int32(0)
            for channel in wanted:
                taken = jnp.where(channel == c, 1, taken)
            ranks.append(jnp.where(taken == 1, -1, free))
            free = free + 1 - taken
        line, spare = [], jnp.int32(0)
        for place in range(channels):
            filler = jnp.int32(0)
            for c in range(channels):
                filler = jnp.where(ranks[c] == spare, c, filler)
            if place < rounds:
                repeated = jnp.where(first[place] == place, 0, 1)
                line.append(jnp.where(repeated == 1, filler, wanted[place]))
                spare = spare + repeated
            else:
                line.append(filler)
                spare = spare + 1
        return wanted, first, line

    barrier = pltpu.get_barrier_semaphore()
    edge = jnp.zeros((16, BLOCK), jnp.bfloat16)
    edges = [*range(0, halo, 16), *range(size, rows, 16)]
    for at in edges:
        for step in range(rounds):
            for side in range(2):
                for zz in range(QUAD):
                    held_ref[step, side, zz, at : at + 16, :] = edge
        for c in range(channels):
            pair_ref[c, at : at + 16, :] = edge
            own_ref[c, at : at + 16, :] = edge
    peers = [{"chan": pair_z * 2 + y}, {"chan": far[0] * 2 + y}, {"chan": far[1] * 2 + y}, {"chan": z * 2 + 1 - y}]
    peers += [{"win": lax.rem(win + 1 + step, rounds)} for step in range(rounds - 1)]
    for peer in peers:
        pl.semaphore_signal(barrier, inc=1, device_id=peer, device_id_type=MESH)

    def near_copy(place):
        return pltpu.make_async_remote_copy(
            src_ref=near_ref.at[place],
            dst_ref=pair_ref.at[place, held_rows(1 - half), :],
            send_sem=pair_sem.at[0, place],
            recv_sem=pair_sem.at[1, place],
            device_id=peers[0],
            device_id_type=MESH,
        )

    def near_wait(place):
        pltpu.make_async_remote_copy(
            src_ref=near_ref.at[place],
            dst_ref=pair_ref.at[place, held_rows(half), :],
            send_sem=pair_sem.at[0, place],
            recv_sem=pair_sem.at[1, place],
            device_id=peers[0],
            device_id_type=MESH,
        ).wait_recv()

    def far_copy(step, k):
        return pltpu.make_async_remote_copy(
            src_ref=pick_ref.at[step, source_rows(k), :],
            dst_ref=held_ref.at[step, 0, z, held_rows(k), :],
            send_sem=far_send.at[step, k],
            recv_sem=far_recv.at[step, half],
            device_id=peers[1 + k],
            device_id_type=MESH,
        )

    def far_wait(step, k):
        pltpu.make_async_remote_copy(
            src_ref=pick_ref.at[step, source_rows(half), :],
            dst_ref=held_ref.at[step, 0, far[k], held_rows(half), :],
            send_sem=far_send.at[step, k],
            recv_sem=far_recv.at[step, k],
            device_id=peers[1 + k],
            device_id_type=MESH,
        ).wait_recv()

    def side_copy(step, o):
        return pltpu.make_async_remote_copy(
            src_ref=held_ref.at[step, 0, order[o], held_rows(half), :],
            dst_ref=held_ref.at[step, 1, order[o], held_rows(half), :],
            send_sem=side_send.at[step, o],
            recv_sem=side_recv.at[step, o],
            device_id=peers[3],
            device_id_type=MESH,
        )

    def stack_copy(step, which):
        return pltpu.make_async_remote_copy(
            src_ref=sent_ref.at[step, which],
            dst_ref=land_ref.at[step, which],
            send_sem=stack_send.at[step, which],
            recv_sem=stack_recv.at[step, which],
            device_id={"win": round_at(step)},
            device_id_type=MESH,
        )

    end_copy = pltpu.make_async_remote_copy(
        src_ref=half_ref,
        dst_ref=part_ref,
        send_sem=end_sem.at[0],
        recv_sem=end_sem.at[1],
        device_id=peers[0],
        device_id_type=MESH,
    )

    wanted, _, line = plan(chan)
    for step in range(rounds):
        pick_ref[step] = pieces_ref[wanted[step]]
        held_ref[step, 0, z, held_rows(half), :] = pick_ref[step, source_rows(half), :]
    for place in range(channels):
        near_ref[place] = pieces_ref[line[place], source_rows(1 - half), :]
    pl.semaphore_wait(barrier, len(peers))
    ahead = [1, 2, 5, 8]
    sent = 0
    for step in range(rounds):
        for place in range(sent, ahead[step]):
            near_copy(place).start()
        sent = ahead[step]
        for k in range(2):
            far_copy(step, k).start()
    for step in range(rounds):
        side_copy(step, 0).start()
    for c in range(channels):
        own_ref[c, held_rows(half), :] = pieces_ref[c, source_rows(half), :]

    def twisted(real, imag, f):
        cos, sin = twist_ref[f, 0], twist_ref[f, 1]
        reals, imags = [], []
        for part in range(real.shape[1] // BLOCK):
            lanes = slice(part * BLOCK, (part + 1) * BLOCK)
            turned = []
            for at in range(0, real.shape[0], 8):
                re, im = real[at : at + 8, lanes], imag[at : at + 8, lanes]
                turned.append((re * cos + im * sin, im * cos - re * sin))
            reals.append(jnp.concatenate([t[0] for t in turned], axis=0))
            imags.append(jnp.concatenate([t[1] for t in turned], axis=0))
        return jnp.concatenate(reals, axis=1).astype(jnp.bfloat16), jnp.concatenate(imags, axis=1).astype(jnp.bfloat16)

    def half_turn(value):
        return pltpu.roll(value, BLOCK // 2, 1)

    def spread(refs, at, count, put):
        joined = jnp.concatenate([r[at : at + count, :] for r in refs], axis=1)
        put(jnp.dot(joined, perm_ref[...], preferred_element_type=jnp.float32).astype(jnp.bfloat16))

    def receivers(which, ref, spin_ref):
        for part in range(channels // QUAD):
            def put(value):
                for q in range(QUAD):
                    xa_ref[q, 0:span, part * BLOCK : (part + 1) * BLOCK] = value[:, q * BLOCK : (q + 1) * BLOCK]

            spread([ref.at[part * QUAD + o] for o in range(QUAD)], halo, span, put)

        def waves(g, carry):
            at = pl.multiple_of(g * two * TAPS // QUAD, 16)
            taken = jnp.concatenate([xa_ref[q, pl.ds(at, two * TAPS // QUAD), :] for q in range(QUAD)], axis=0)
            seen = jnp.dot(dft_a_ref[...], taken, preferred_element_type=jnp.float32)
            here = pl.multiple_of(g * two, 16)
            for f in range(TONES):
                real, imag = twisted(seen[2 * f * two : (2 * f + 1) * two], seen[(2 * f + 1) * two : (2 * f + 2) * two], f)
                sa_ref[f, 0, pl.ds(here, two), :] = real
                sa_ref[f, 1, pl.ds(here, two), :] = imag
            return carry

        lax.fori_loop(0, pairs, waves, 0, unroll=8)
        wide = pairs * two

        def turned(f, carry):
            real, imag = [
                lax.dot_general(
                    spin_ref[...], sa_ref[f, v], (((1,), (1,)), ((), ())), preferred_element_type=jnp.float32
                ).astype(jnp.bfloat16)
                for v in range(2)
            ]
            deep = STEP * channels // 2
            for u in range(2):
                at = 2 * u * wide
                re, im = real[u * deep : (u + 1) * deep], imag[u * deep : (u + 1) * deep]
                a_ref[which, f, 0, :, at : at + wide] = re
                a_ref[which, f, 0, :, at + wide : at + 2 * wide] = im
                a_ref[which, f, 1, :, at : at + wide] = -im
                a_ref[which, f, 1, :, at + wide : at + 2 * wide] = re
            return carry

        lax.fori_loop(0, TONES, turned, 0, unroll=12)

    def sources(step):
        wide = pairs * two
        for side in range(2):
            def put(value):
                for q in range(QUAD):
                    xb_ref[q, :, side * BLOCK : (side + 1) * BLOCK] = value[:, q * BLOCK : (q + 1) * BLOCK]

            spread([held_ref.at[step, side, zz] for zz in range(QUAD)], 0, rows, put)

        def waves(g, carry):
            count = windows * (TAPS + POINTS) // QUAD
            at = pl.multiple_of(g * two * TAPS // QUAD, 16)
            taken = jnp.concatenate([xb_ref[q, pl.ds(at, count), :] for q in range(QUAD)], axis=0)
            seen = jnp.dot(dft_b_ref[...], taken, preferred_element_type=jnp.float32)
            here = pl.multiple_of(g * two, 16)
            for f in range(TONES):
                real, imag = twisted(seen[2 * f * two : (2 * f + 1) * two], seen[(2 * f + 1) * two : (2 * f + 2) * two], f)
                for v, part in enumerate((real, imag)):
                    sb_ref[step, f, pl.ds(pl.multiple_of(here + v * wide, 16), two), :] = part
                    for side in range(2):
                        lanes = slice(side * BLOCK, (side + 1) * BLOCK)
                        sb_ref[step, f, pl.ds(pl.multiple_of(here + (v + 2) * wide, 16), two), lanes] = half_turn(part[:, lanes])
            return carry

        lax.fori_loop(0, pairs, waves, 0, unroll=8)

    def products(step, which):
        def tone(f, carry):
            right = sb_ref[step, f]
            sums = []
            for v in range(2):
                seen = jnp.dot(a_ref[which, f, v], right, preferred_element_type=jnp.float32)
                for side in range(2):
                    lanes = slice(side * BLOCK, (side + 1) * BLOCK)
                    total = [None] * 4
                    for i in range(STEP // 2):
                        term = seen[i * channels : (i + 1) * channels, lanes]
                        if i:
                            term = pltpu.roll(term, BLOCK - QUAD * i, 1)
                        total[i % 4] = term if total[i % 4] is None else total[i % 4] + term
                    sums.append((total[0] + total[1]) + (total[2] + total[3]))
            cos, sin = twist_ref[f, 0], twist_ref[f, 1]
            at = pl.multiple_of(f * 2 * channels, 16)
            for side in range(2):
                lanes = slice(side * BLOCK, (side + 1) * BLOCK)
                re, im = sums[side], sums[2 + side]
                both = jnp.concatenate([re * cos - im * sin, re * sin + im * cos], axis=0)
                spec_ref[which, pl.ds(at, 2 * channels), lanes] = both
            return carry

        lax.fori_loop(0, TONES, tone, 0, unroll=12)
        rows = inverse_ref.shape[0] // 2
        seen = spec_ref[which]
        high = seen.astype(jnp.bfloat16)
        low = (seen - high.astype(jnp.float32)).astype(jnp.bfloat16)
        sums = jnp.dot(inverse_ref[...], high, preferred_element_type=jnp.float32)
        sums = sums[:rows] + sums[rows:] + jnp.dot(inverse_ref[:rows], low, preferred_element_type=jnp.float32)
        sums = sums[: LAGS * channels]
        sums = jnp.concatenate([sums[:, :BLOCK], sums[:, BLOCK:]], axis=0)
        res_ref[which] = sums
        sent_ref[step, which] = sums.astype(jnp.bfloat16)

    _, first, pair_line = plan(pair_z * 2 + y)

    def pass_on(step):
        if step < 3:
            near_wait(step)
        total = pair_ref[0, held_rows(half), :]
        if step:
            total = jnp.zeros(total.shape, jnp.float32)
            for place in range(step + 1):
                share = jnp.where(first[step] == place, 1.0, 0.0)
                total = total + pair_ref[place, held_rows(half), :].astype(jnp.float32) * share
            total = total.astype(jnp.bfloat16)
        held_ref[step, 0, pair_z, held_rows(half), :] = total
        side_copy(step, 1).start()
        for k in range(2):
            far_wait(step, k)
            side_copy(step, 2 + k).start()

    def take(step):
        for o in range(QUAD):
            side_copy(step, o).wait_recv()
        sources(step)

    xa_ref[:, span:, :] = jnp.zeros((QUAD, xa_ref.shape[1] - span, xa_ref.shape[2]), jnp.bfloat16)
    receivers(0, own_ref, turn_ref)
    row = lax.broadcasted_iota(jnp.int32, spun_ref.shape, 0)
    lane = lax.broadcasted_iota(jnp.int32, spun_ref.shape, 1)
    place = lane // BLOCK * QUAD + lane % QUAD
    meant = jnp.zeros_like(lane)
    for c in range(channels):
        meant = jnp.where(place == c, pair_line[c], meant)
    hit = (lane % BLOCK // QUAD * channels + meant) == row
    spun_ref[...] = jnp.where(hit, 1.0, 0.0).astype(jnp.bfloat16)
    pass_on(0)
    pass_on(1)

    def early(step, carry):
        take(step)
        products(step, 0)
        stack_copy(step, 0).start()

        @pl.when(step == 0)
        def _():
            pass_on(2)

        return carry

    lax.fori_loop(0, 2, early, 0)
    for place in range(3, channels):
        near_wait(place)
    receivers(1, pair_ref, spun_ref)

    def shared(step, carry):
        products(step, 1)
        stack_copy(step, 1).start()

        @pl.when(step == 0)
        def _():
            pass_on(3)

        return carry

    lax.fori_loop(0, 2, shared, 0)

    def summed(which):
        total = res_ref[which]
        for step in range(rounds - 1):
            stack_copy(step, which).wait_recv()
            total = total + land_ref[step, which].astype(jnp.float32)
        return total

    def late(step, carry):
        take(step)

        def each(index, carry):
            products(step, 1 - index)

            @pl.when(step < rounds - 1)
            def _():
                stack_copy(step, 1 - index).start()

            @pl.when((step == rounds - 1) & (index == 0))
            def _():
                half_ref[...] = summed(1).astype(jnp.bfloat16)
                end_copy.start()

            return carry

        lax.fori_loop(0, 2, each, 0)
        return carry

    lax.fori_loop(2, rounds, late, 0)
    whole_sum = summed(0)
    for step in range(rounds):
        for k in range(2):
            far_copy(step, k).wait_send()
        for o in range(QUAD):
            side_copy(step, o).wait_send()
    for place in range(channels):
        near_copy(place).wait_send()
    for step in range(rounds - 1):
        for which in range(2):
            stack_copy(step, which).wait_send()
    end_copy.wait_recv()
    both = whole_sum + part_ref[...].astype(jnp.float32)
    groups = (LAGS - 1) // QUAD
    for side in range(2):
        total = both[side * LAGS * channels : (side + 1) * LAGS * channels]
        lined = jnp.concatenate(
            [
                jnp.concatenate(
                    [total[(QUAD * g + q) * channels : (QUAD * g + q + 1) * channels] for g in range(groups)], axis=0
                )
                for q in range(QUAD)
            ],
            axis=1,
        )
        high = lined.astype(jnp.bfloat16)
        rest = lined - high.astype(jnp.float32)
        middle = rest.astype(jnp.bfloat16)
        low = (rest - middle.astype(jnp.float32)).astype(jnp.bfloat16)
        split = [
            lax.dot_general(p, perm_ref[...], (((1,), (1,)), ((), ())), preferred_element_type=jnp.float32)
            for p in (high, middle, low)
        ]
        whole = split[0] + split[1] + split[2]
        last = total[(LAGS - 1) * channels : LAGS * channels]
        for zz in range(QUAD):
            for g in range(groups):
                fin_ref[side * QUAD + zz, :, g * BLOCK : (g + 1) * BLOCK] = whole[
                    g * channels : (g + 1) * channels, zz * BLOCK : (zz + 1) * BLOCK
                ]
            fin_ref[side * QUAD + zz, :, groups * BLOCK : (groups + 1) * BLOCK] = jnp.broadcast_to(
                last[:, zz : zz + 1], (channels, BLOCK)
            )
    for i in range(per_round):
        shard = sources_ref[win, i] // channels
        side = jnp.where(shard - 2 * (shard // 2) == y, 0, 1)
        out_ref[i] = fin_ref[side * QUAD + shard // 2][:, : out_ref.shape[2]]
    end_copy.wait_send()


def halves_fit(channels, windows, blocks, rounds, per_round):
    chan_size, win_size = lax.axis_size("chan"), lax.axis_size("win")
    return (
        rounds == win_size
        and per_round == chan_size
        and chan_size == 2 * QUAD
        and win_size == QUAD
        and channels == 2 * QUAD
        and windows == 8
        and blocks % 4 == 0
    )


def correlate_halves(pieces, sources, factor):
    channels, depth, _ = pieces.shape
    rounds, per_round = sources.shape
    windows = 8
    tables = constants(windows, channels, factor)
    span = depth // 2
    pairs = -(-span // (windows * 4))
    rows = (pairs * 4 + 2 * HALO) * windows
    wide = channels * STEP
    stack = (2 * LAGS * channels, BLOCK)
    bf16, f32 = jnp.bfloat16, jnp.float32
    dma = pltpu.SemaphoreType.DMA
    return pl.pallas_call(
        functools.partial(halves_kernel, windows),
        out_shape=jax.ShapeDtypeStruct((per_round, channels, 2 * MAX_LAG + 1), f32),
        in_specs=[pl.BlockSpec(memory_space=pltpu.VMEM), pl.BlockSpec(memory_space=pltpu.SMEM)]
        + [pl.BlockSpec(memory_space=pltpu.VMEM)] * len(tables),
        out_specs=pl.BlockSpec(memory_space=pltpu.VMEM),
        scratch_shapes=[
            pltpu.VMEM((channels, span + HALO * windows, BLOCK), bf16),
            pltpu.VMEM((channels, rows, BLOCK), bf16),
            pltpu.VMEM((channels, rows, BLOCK), bf16),
            pltpu.VMEM((rounds, depth, BLOCK), bf16),
            pltpu.VMEM((rounds, 2, QUAD, rows, BLOCK), bf16),
            pltpu.VMEM((wide, wide), bf16),
            pltpu.VMEM((QUAD, pairs * 4 * windows, wide), bf16),
            pltpu.VMEM((TONES, 2, pairs * 2 * windows, wide), bf16),
            pltpu.VMEM((2, TONES, 2, wide // 2, pairs * 8 * windows), bf16),
            pltpu.VMEM((QUAD, rows, 2 * BLOCK), bf16),
            pltpu.VMEM((rounds, TONES, pairs * 8 * windows, 2 * BLOCK), bf16),
            pltpu.VMEM((2, TONES * 2 * channels, 2 * BLOCK), f32),
            pltpu.VMEM((2, *stack), f32),
            pltpu.VMEM((rounds, 2, *stack), bf16),
            pltpu.VMEM((rounds - 1, 2, *stack), bf16),
            pltpu.VMEM(stack, bf16),
            pltpu.VMEM(stack, bf16),
            pltpu.VMEM((per_round, channels, 2 * MAX_LAG + BLOCK), f32),
            dma((2, channels)),
            dma((rounds, 2)),
            dma((rounds, 2)),
            dma((rounds, QUAD)),
            dma((rounds, QUAD)),
            dma((rounds - 1, 2)),
            dma((rounds - 1, 2)),
            dma((2,)),
        ],
        compiler_params=pltpu.CompilerParams(
            vmem_limit_bytes=48 * 1024 * 1024, collective_id=1, has_side_effects=True
        ),
    )(pieces, sources, *tables)


def on_device(strain, sources):
    channels, windows, samples = strain.shape
    rounds, per_round = sources.shape
    total_sources = rounds * per_round
    factor = 1.0 / math.sqrt(lax.axis_size("win") * windows * samples)
    blocks = -(-samples // BLOCK)
    while blocks * windows % 16:
        blocks += 1
    depth = blocks * windows

    whitened = whiten(strain)
    padded = jnp.pad(whitened, ((0, 0), (0, 0), (0, blocks * BLOCK - samples)))
    pieces = padded.reshape(channels, windows, blocks, BLOCK)
    pieces = jnp.transpose(pieces, (0, 2, 1, 3)).reshape(channels, depth, BLOCK)

    if halves_fit(channels, windows, blocks, rounds, per_round):
        return correlate_halves(pieces, sources.astype(jnp.int32), factor)

    flat_sources = sources.reshape(-1)
    per_shard = total_sources // lax.axis_size("chan")
    owner = flat_sources // channels
    position = jnp.arange(total_sources)
    earlier = (owner[None, :] == owner[:, None]) & (position[None, :] < position[:, None])
    rank = jnp.sum(earlier.astype(jnp.int32), axis=1)
    me = lax.axis_index("chan")
    mine = owner == me
    slot_pick = (mine[None, :] & (rank[None, :] == jnp.arange(per_shard)[:, None])).astype(jnp.int32)
    local_channel = jnp.sum(slot_pick * (flat_sources - me * channels)[None, :], axis=1)
    order = (owner * per_shard + rank).astype(jnp.int32)

    return correlate(pieces, local_channel.astype(jnp.int32), order, windows, rounds, factor)


def solution(mesh):
    in_specs = (P("chan", "win", None), P())
    out_specs = P("win", "chan", None)
    return jax.shard_map(
        on_device, mesh=mesh, in_specs=in_specs, out_specs=out_specs, check_vma=False
    )
```
